32 devices in a mesh: sib: 2 (over core), row: 4 (over z), col: 4 (over y, x).
Axes of the slice: x: 2, y: 2, z: 4, core: 2. Of those that a mesh axis runs over, the one named last changes fastest.
Arguments:
- front: float32 [8192, 8192], P('row', 'col'), may hold values from -4 to 4
- child_updates: float32 [2, 8192, 8192], P('sib', ('row', 'col')), may hold values from -2 to 2
- child_map: int32 [2, 64], P('sib'), may hold values from 0 to 63, as said below
- pivot_inverses: float32 [3, 512, 512], replicated, may hold values from -0.0029296875 to 0.0029296875
Outputs:
- factored: float32 [8192, 8192], P('row', 'col')
The draws below stay inside these ranges and needn't reach their ends.
Inputs may be any that keep to these rules, and one draw needn't show every extreme that they name: Each child_map[c] is a permutation of the 64 front blocks. Of the 16 child blocks i that share i // 16, every value of child_map[c, i] // 16 that occurs occurs exactly 4 times.
All inputs are finite; a program needn't handle non-finite values.
Results may differ from the reference program's by a relative error of at most 0.0001.
Values sent between devices are 32-bit elements; how exact they have to be, the bound alone decides.
No kernel may reach another device: no remote copies, remote signals or barrier semaphores. Data moves between devices by JAX's collectives and lax.ppermute only.
A program may use at most 192 MiB of HBM per device.

```python
import jax
import jax.numpy as jnp
from jax import lax

F = 8192
W = 512
BLK = 128
NP = 3
FB = 64


def reverse_bits(values, bit_count):
    result = jnp.zeros_like(values)
    for bit in range(bit_count):
        result = result | (values >> bit & 1) << bit_count - 1 - bit
    return result


def draw_child_map(key, part):
    key = jax.random.fold_in(key, 23)
    bit_count = FB.bit_length() - 1
    block_ids = jnp.arange(FB, dtype=jnp.int32)
    child_maps = []
    for which_child in range(2):
        child_key = jax.random.fold_in(key, 17 + which_child)
        key_before, key_after = jax.random.split(child_key, 2)
        before = jax.random.randint(key_before, (), 0, FB, dtype=jnp.int32)
        after = jax.random.randint(key_after, (), 0, FB, dtype=jnp.int32)
        mixed = jnp.bitwise_xor(block_ids, before)
        child_maps.append(jnp.bitwise_xor(reverse_bits(mixed, bit_count), after))
    return jnp.stack(child_maps).astype(jnp.int32)


def levels(key, shape, shards, low, largest):
    gain, own = 1.0, jax.random.fold_in(key, 6)
    for position, parts in shards:
        heights = jnp.exp(jax.random.uniform(jax.random.fold_in(own, position), (parts,), jnp.float32, low / len(shards), largest / len(shards)))
        gain = gain * jnp.repeat(heights, shape[position] // parts).reshape([-1 if axis == position else 1 for axis in range(len(shape))])
    return gain


def centred(key, dims, deviation, bound, pieces=(), kind=jnp.bfloat16):
    level = levels(key, dims, pieces, -0.22, 0.18) if pieces else 1.0
    entries = jax.random.normal(key, dims, jnp.float32) * deviation * level
    return jnp.minimum(jnp.maximum(entries, -bound), bound).astype(kind)


def setup_inputs(seed: int = 0) -> dict:
    key_of = jax.random.split(jax.random.key(seed), 5)
    return {
        "front": centred(key_of[0], (F, F), 1.0, 4.0, ((0, 4), (1, 4)), jnp.float32),
        "child_updates": centred(key_of[1], (2, F, F), 0.5, 2.0, ((0, 2), (1, 16)), jnp.float32),
        "child_map": draw_child_map(jax.random.fold_in(key_of[4], 71), 0),
        "pivot_inverses": centred(key_of[3], (NP, W, W), (16 * W * W) ** -0.5, 0.0029296875, (), jnp.float32),
    }


def reference(front, child_updates, child_map, pivot_inverses):
    working = front
    positions = jnp.arange(F, dtype=jnp.int32)
    for which_child in range(2):
        inverse_map = jnp.argsort(child_map[which_child]).astype(jnp.int32)
        source_index = (inverse_map[positions // BLK] * BLK + positions % BLK).astype(jnp.int32)
        update_rows = jnp.take(child_updates[which_child], source_index, axis=0)
        working = working + jnp.take(update_rows, source_index, axis=1)
    for panel_index in range(NP):
        first_col = panel_index * W
        after_panel = first_col + W
        panel_block = jnp.dot(working[:, first_col:after_panel], pivot_inverses[panel_index], precision=lax.Precision.HIGHEST, preferred_element_type=jnp.float32)
        pivot_rows = working[first_col:after_panel, after_panel:]
        trailing = jnp.dot(panel_block[after_panel:], pivot_rows, precision=lax.Precision.HIGHEST, preferred_element_type=jnp.float32)
        working = working.at[after_panel:, after_panel:].add(-trailing)
        working = working.at[:, first_col:after_panel].set(panel_block)
    return working
```

```python
import jax
import jax.numpy as jnp
from jax import lax
from jax.experimental import pallas as pl
from jax.experimental.pallas import tpu as pltpu
from jax.sharding import PartitionSpec as P

F = 8192
W = 512
BLK = 128
NP = 3
CHUNKS = (4, 4, 4, 2, 2)
VMEM_LIMIT = 48 * 1024 * 1024
TRAIL = lax.Precision.HIGH


def dot(a, b, precision):
    return jnp.dot(a, b, precision=precision, preferred_element_type=jnp.float32)


def call(kernel, tables, arrays, outs, scratch, read, written):
    return pl.pallas_call(
        kernel,
        out_shape=[jax.ShapeDtypeStruct(shape, jnp.float32) for shape in outs],
        in_specs=[pl.BlockSpec(memory_space=pltpu.SMEM)] * len(tables)
        + [pl.BlockSpec(memory_space=pl.ANY)] * len(arrays),
        out_specs=[pl.BlockSpec(memory_space=pl.ANY)] * len(outs),
        scratch_shapes=scratch,
        compiler_params=pltpu.CompilerParams(vmem_limit_bytes=VMEM_LIMIT),
        cost_estimate=pl.CostEstimate(
            flops=0, bytes_accessed=4 * (read + written), transcendentals=0
        ),
    )(*tables, *arrays)


def split_columns(child, table, first, count, parts):
    rows = child.shape[0]
    stride = table.shape[0] // parts

    def kernel(table_ref, child_ref, *rest):
        outs, sems = rest[:parts], rest[parts]
        copies = []
        for part in range(parts):
            for b in range(count):
                source = pl.multiple_of(table_ref[part * stride + first + b] * BLK, BLK)
                copies.append(
                    pltpu.make_async_copy(
                        child_ref.at[:, pl.ds(source, BLK)],
                        outs[part].at[:, pl.ds(b * BLK, BLK)],
                        sems.at[part * count + b],
                    )
                )
                copies[-1].start()
        for copy in copies:
            copy.wait()

    size = rows * count * BLK * parts
    return call(
        kernel,
        [table],
        [child],
        [(rows, count * BLK)] * parts,
        [pltpu.SemaphoreType.DMA((parts * count,))],
        size,
        size,
    )


def order_rows(sources, codes):
    rows, width = sources[0].shape
    per = rows // BLK
    total = codes.shape[0]

    def kernel(code_ref, *rest):
        ins, out, sems = rest[: len(sources)], rest[len(sources)], rest[len(sources) + 1]
        for o in range(total):
            code = code_ref[o]
            which = code // per
            start = pl.multiple_of((code % per) * BLK, BLK)
            for s in range(len(sources)):

                @pl.when(which == s)
                def _(s=s, o=o, start=start):
                    pltpu.make_async_copy(
                        ins[s].at[pl.ds(start, BLK)], out.at[pl.ds(o * BLK, BLK)], sems.at[o]
                    ).start()

        for o in range(total):
            pltpu.make_async_copy(
                ins[0].at[pl.ds(0, BLK)], out.at[pl.ds(o * BLK, BLK)], sems.at[o]
            ).wait()

    size = total * BLK * width
    return call(
        kernel,
        [codes],
        list(sources),
        [(total * BLK, width)],
        [pltpu.SemaphoreType.DMA((total,))],
        size,
        size,
    )[0]


def assemble(front, own, other, tables, first, half_rows):
    rows, width = own.shape
    blocks = rows // BLK

    def kernel(table_ref, front_ref, own_ref, other_ref, out, half, fbuf, abuf, bbuf, sems, osem):
        def copies(o):
            here = pl.ds(o * BLK, BLK)
            a = pl.multiple_of(table_ref[o] * BLK, BLK)
            b = pl.multiple_of(table_ref[blocks + o] * BLK, BLK)
            return (
                pltpu.make_async_copy(
                    front_ref.at[here, pl.ds(first, width)], fbuf.at[here], sems.at[0, o]
                ),
                pltpu.make_async_copy(own_ref.at[pl.ds(a, BLK)], abuf.at[here], sems.at[1, o]),
                pltpu.make_async_copy(other_ref.at[pl.ds(b, BLK)], bbuf.at[here], sems.at[2, o]),
            )

        for o in range(blocks):
            for copy in copies(o):
                copy.start()
        back = []
        for o in range(blocks):
            for copy in copies(o):
                copy.wait()
            here = pl.ds(o * BLK, BLK)
            fbuf[here, :] = (abuf[here, :] + bbuf[here, :]) + fbuf[here, :]
            back.append(pltpu.make_async_copy(fbuf.at[here], out.at[here], sems.at[0, o]))
            back[-1].start()
        mine = pl.multiple_of(table_ref[2 * blocks] * half_rows, BLK)
        last = pltpu.make_async_copy(fbuf.at[pl.ds(mine, half_rows)], half, osem)
        last.start()
        for copy in back:
            copy.wait()
        last.wait()

    size = rows * width
    return call(
        kernel,
        [tables],
        [front, own, other],
        [(rows, width), (half_rows, width)],
        [pltpu.VMEM((rows, width), jnp.float32)] * 3
        + [pltpu.SemaphoreType.DMA((3, blocks)), pltpu.SemaphoreType.DMA],
        3 * size,
        size + half_rows * width,
    )


def block_tables(mapping, group):
    total = mapping.shape[0]
    ids = jnp.arange(total, dtype=jnp.int32)
    inverse = jnp.sum(jnp.where(mapping[:, None] == ids[None, :], ids[:, None], 0), axis=0)
    target = mapping // group
    same = (
        (ids[:, None] // group == ids[None, :] // group)
        & (target[:, None] == target[None, :])
        & (ids[None, :] < ids[:, None])
    )
    return inverse, target, jnp.sum(same.astype(jnp.int32), axis=1)


def halves(mine, theirs, sib):
    low = jnp.where(sib == 0, mine, theirs)
    high = jnp.where(sib == 0, theirs, mine)
    return low, high


def local(front, child_updates, child_map, pivot_inverses):
    n_row, n_col = lax.axis_size("row"), lax.axis_size("col")
    row, col, sib = lax.axis_index("row"), lax.axis_index("col"), lax.axis_index("sib")
    rows, cols = front.shape
    child = child_updates[0]
    group, cgroup, per = rows // BLK, cols // BLK, child.shape[0] // BLK
    capacity = group // n_row
    pivots = NP * W
    swap = [(0, 1), (1, 0)]

    inverse, target, rank = block_tables(child_map[0], group)
    shift_to = (col + jnp.arange(n_col, dtype=jnp.int32)) % n_col
    column_table = inverse.reshape(n_col, cgroup)[shift_to].reshape(-1)
    ids = jnp.arange(group, dtype=jnp.int32)
    own = row * group + ids
    slot = target[own] * capacity + rank[own]
    source = jnp.sum(jnp.where(slot[None, :] == ids[:, None], ids[None, :], 0), axis=1)
    codes = (col - source // per) % n_col * per + source % per
    arriving = inverse[own]
    place = arriving // group * capacity + rank[arriving]
    place_other = lax.ppermute(place, "sib", swap)
    place_tables = jnp.concatenate([place, place_other, sib[None].astype(jnp.int32)])

    steps = n_col.bit_length() - 1
    order = [[1 << b for b in reversed(range(steps))], [1 << b for b in range(steps)]]

    def spread_panel(value):
        held = [{0}, {0}]
        for step in range(steps):
            pairs, fresh = [], []
            for core in range(2):
                bit = order[core][step]
                new = {h | bit for h in held[core]}
                pairs += [(core * n_col + h, core * n_col + (h | bit)) for h in sorted(held[core])]
                fresh.append(sorted(new))
                held[core] |= new
            got = lax.ppermute(value, ("sib", "col"), pairs)
            hit = jnp.zeros((), jnp.bool_)
            for core in range(2):
                for h in fresh[core]:
                    hit = hit | ((sib == core) & (col == h))
            value = jnp.where(hit, got, value)
        return value

    first = 0
    received = []
    for count in CHUNKS:
        parts = split_columns(child, column_table, first, count, n_col)
        got = [parts[0]]
        for s in range(1, n_col):
            got.append(lax.ppermute(parts[s], "col", [(i, (i + s) % n_col) for i in range(n_col)]))
        received.append(got)
        first += count

    A, R, U = [], [], []
    first = 0
    for got, count in zip(received, CHUNKS):
        outgoing = order_rows(got, codes)
        mine = lax.all_to_all(
            outgoing.reshape(n_row, -1, count * BLK), "row", split_axis=0, concat_axis=0, tiled=True
        ).reshape(rows, count * BLK)
        theirs = lax.ppermute(mine, "sib", swap)
        whole, half = assemble(front, mine, theirs, place_tables, first * BLK, pivots // 2)
        A.append(whole)
        hop, kept = half, half
        for step in range(1, n_row):
            hop = lax.ppermute(hop, "row", [(step - 1, step)])
            kept = jnp.where(row == step, hop, kept)
        low, high = halves(kept, lax.ppermute(kept, "sib", swap), sib)
        both = jnp.concatenate([low, high], axis=0)
        R.append([both[k * W : (k + 1) * W] for k in range(NP)])
        first += count

    corner, lower = [], []
    half_own = rows // 2
    row_ids = row * rows + jnp.arange(rows, dtype=jnp.int32)

    def eliminate(j, k):
        pivot = R[j][k]
        for later in range(k + 1, NP):
            R[j][later] = R[j][later] - dot(corner[k][later], pivot, TRAIL)

    final = []
    for k in range(NP):
        for earlier in range(k):
            eliminate(k, earlier)
        work = A[k]
        if k:
            work = work - dot(
                jnp.concatenate(lower[:k], axis=1), jnp.concatenate(R[k][:k], axis=0), TRAIL
            )
        A[k] = work
        pieces = [lax.dynamic_slice_in_dim(work, sib * half_own, half_own, 0)]
        below = pivots - (k + 1) * W
        if below:
            rest = jnp.concatenate(R[k][k + 1 :], axis=0)
            pieces.append(lax.dynamic_slice_in_dim(rest, sib * (below // 2), below // 2, 0))
        panel = dot(jnp.concatenate(pieces, axis=0), pivot_inverses[k], lax.Precision.HIGHEST)
        panel = spread_panel(panel)
        low, high = halves(panel, lax.ppermute(panel, "sib", swap), sib)
        final.append(jnp.concatenate([low[:half_own], high[:half_own]], axis=0))
        lower.append(jnp.where((row_ids >= (k + 1) * W)[:, None], final[-1], 0.0))
        rest = jnp.concatenate([low[half_own:], high[half_own:]], axis=0)
        corner.append(
            {later: rest[(later - k - 1) * W : (later - k) * W] for later in range(k + 1, NP)}
        )

    outs = []
    for j in range(len(CHUNKS)):
        done = j if j < NP else 0
        for k in range(done, NP):
            eliminate(j, k)
        update = dot(
            jnp.concatenate(lower[done:], axis=1), jnp.concatenate(R[j][done:], axis=0), TRAIL
        )
        value = A[j] - update
        outs.append(jnp.where(col == 0, final[j], value) if j < NP else value)
    return jnp.concatenate(outs, axis=1)


def spread(value, axis, source):
    kept = jnp.where(lax.axis_index(axis) == source, value, 0).astype(value.dtype)
    return lax.psum(kept, axis)


def plain_local(front, child_updates, child_map, pivot_inverses):
    row_count = lax.axis_size("row")
    row_here = lax.axis_index("row")
    col_here = lax.axis_index("col")
    sib_here = lax.axis_index("sib")
    rows_dev, cols_dev = front.shape
    group_blocks = rows_dev // BLK
    total_blocks = child_map.shape[1]
    capacity = max(1, group_blocks * group_blocks // total_blocks)
    inverse_map, target_group, rank_of = block_tables(child_map[0], group_blocks)
    columns = jnp.arange(F, dtype=jnp.int32)
    column_source = inverse_map[columns // BLK] * BLK + columns % BLK
    permuted = jnp.take(child_updates[0], column_source, axis=1)
    group_rows = lax.all_to_all(permuted, "col", split_axis=1, concat_axis=0, tiled=True)
    local_blocks = group_rows.reshape(group_blocks, BLK, cols_dev)
    local_ids = jnp.arange(group_blocks, dtype=jnp.int32)
    own_blocks = row_here * group_blocks + local_ids
    send_slot = target_group[own_blocks] * capacity + rank_of[own_blocks]
    slot_ids = jnp.arange(row_count * capacity, dtype=jnp.int32)
    slot_hits = send_slot[None, :] == slot_ids[:, None]
    source_block = jnp.sum(jnp.where(slot_hits, local_ids[None, :], 0), axis=1)
    filled = jnp.any(slot_hits, axis=1)
    outgoing = jnp.where(filled[:, None, None], jnp.take(local_blocks, source_block, axis=0), 0.0)
    incoming = lax.all_to_all(
        outgoing.reshape(row_count * capacity * BLK, cols_dev),
        "row",
        split_axis=0,
        concat_axis=0,
        tiled=True,
    )
    arriving = inverse_map[own_blocks]
    receive_slot = arriving // group_blocks * capacity + rank_of[arriving]
    relocated = jnp.take(
        incoming.reshape(row_count * capacity, BLK, cols_dev), receive_slot, axis=0
    ).reshape(rows_dev, cols_dev)
    half_rows = rows_dev // 2
    working = lax.psum_scatter(
        relocated, "sib", scatter_dimension=0, tiled=True
    ) + lax.dynamic_slice_in_dim(front, sib_here * half_rows, half_rows, 0)
    row_start = row_here * rows_dev + sib_here * half_rows
    global_rows = row_start + jnp.arange(working.shape[0], dtype=jnp.int32)
    global_cols = col_here * cols_dev + jnp.arange(cols_dev, dtype=jnp.int32)
    for panel_index in range(NP):
        first_col = panel_index * W
        after_panel = first_col + W
        col_root = first_col // cols_dev
        col_offset = first_col % cols_dev
        pivot_cols = working[:, col_offset : col_offset + W]
        pivot_cols = spread(pivot_cols, "col", col_root)
        group_offset = first_col % rows_dev
        row_root = group_offset // half_rows * row_count + first_col // rows_dev
        row_offset = group_offset % half_rows
        pivot_rows = spread(working[row_offset : row_offset + W, :], ("sib", "row"), row_root)
        panel_block = jnp.dot(
            pivot_cols,
            pivot_inverses[panel_index],
            precision=lax.Precision.HIGHEST,
            preferred_element_type=jnp.float32,
        )
        update = jnp.dot(
            panel_block,
            pivot_rows,
            precision=lax.Precision.HIGHEST,
            preferred_element_type=jnp.float32,
        )
        inside = (global_rows >= after_panel)[:, None] & (global_cols >= after_panel)[None, :]
        working = working - jnp.where(inside, update, 0.0)
        placed = lax.dynamic_update_slice(working, panel_block, (0, col_offset))
        working = jnp.where(col_here == col_root, placed, working)
    working = lax.all_gather(working, "sib", axis=0, tiled=True)
    return working

def solution(mesh):
    placed = (P("row", "col"), P("sib", ("row", "col"), None), P("sib", None), P())
    rows, cols = F // mesh.shape["row"], F // mesh.shape["col"]
    wide = rows >= NP * W and cols == sum(CHUNKS) * BLK and mesh.shape["sib"] == 2
    return jax.shard_map(
        local if wide else plain_local,
        mesh=mesh,
        in_specs=placed,
        out_specs=P("row", "col"),
        check_vma=False,
    )
```

```python
import jax
import jax.numpy as jnp
from jax import lax
from jax.experimental import pallas as pl
from jax.experimental.pallas import tpu as pltpu
from jax.sharding import PartitionSpec as P

F = 8192
W = 512
BLK = 128
NP = 3
CHUNKS = (4, 4, 4, 2, 2)
VMEM_LIMIT = 48 * 1024 * 1024
TRAIL = lax.Precision.HIGH
PANEL = lax.Precision.HIGHEST


def dot(a, b, precision):
    return jnp.dot(a, b, precision=precision, preferred_element_type=jnp.float32)


TOKEN = (8, 128)


def call(kernel, after, tables, arrays, outs, scratch):
    def ordered(*refs):
        n = len(tables) + len(arrays)
        m = n + len(after)
        kernel(*refs[:n], *refs[m : m + len(outs)], *refs[m + 1 + len(outs) :])

    return pl.pallas_call(
        ordered,
        out_shape=[jax.ShapeDtypeStruct(shape, jnp.float32) for shape in (*outs, TOKEN)],
        in_specs=[pl.BlockSpec(memory_space=pltpu.SMEM)] * len(tables)
        + [pl.BlockSpec(memory_space=pl.ANY)] * (len(arrays) + len(after)),
        out_specs=[pl.BlockSpec(memory_space=pl.ANY)] * (len(outs) + 1),
        scratch_shapes=scratch,
        compiler_params=pltpu.CompilerParams(vmem_limit_bytes=VMEM_LIMIT),
        cost_estimate=pl.CostEstimate(flops=0, bytes_accessed=4096, transcendentals=0),
    )(*tables, *arrays, *after)


def hold(after, value):
    def kernel(value_ref, after_ref, out, token):
        pass

    return pl.pallas_call(
        kernel,
        out_shape=[
            jax.ShapeDtypeStruct(value.shape, jnp.float32),
            jax.ShapeDtypeStruct(TOKEN, jnp.float32),
        ],
        in_specs=[pl.BlockSpec(memory_space=pl.ANY)] * 2,
        out_specs=[pl.BlockSpec(memory_space=pl.ANY)] * 2,
        input_output_aliases={0: 0},
        cost_estimate=pl.CostEstimate(flops=0, bytes_accessed=4096, transcendentals=0),
    )(value, after)


def split_columns(after, child, table, first, count, parts):
    rows = child.shape[0]
    stride = table.shape[0] // parts

    def kernel(table_ref, child_ref, *rest):
        outs, (buf, sems, osems) = rest[:parts], rest[parts:]
        into, back = [], []
        for part in range(parts):
            for b in range(count):
                source = pl.multiple_of(table_ref[part * stride + first + b] * BLK, BLK)
                into.append(
                    pltpu.make_async_copy(
                        child_ref.at[:, pl.ds(source, BLK)],
                        buf.at[part, :, pl.ds(b * BLK, BLK)],
                        sems.at[part * count + b],
                    )
                )
                into[-1].start()
        for part in range(parts):
            for b in range(count):
                into[part * count + b].wait()
            back.append(pltpu.make_async_copy(buf.at[part], outs[part], osems.at[part]))
            back[-1].start()
        for copy in back:
            copy.wait()

    return call(
        kernel,
        after,
        [table],
        [child],
        [(rows, count * BLK)] * parts,
        [
            pltpu.VMEM((parts, rows, count * BLK), jnp.float32),
            pltpu.SemaphoreType.DMA((parts * count,)),
            pltpu.SemaphoreType.DMA((parts,)),
        ],
    )


def order_rows(after, sources, codes):
    rows, width = sources[0].shape
    per = rows // BLK
    total = codes.shape[0]

    def kernel(code_ref, *rest):
        ins, (out, buf, sems, osems) = rest[: len(sources)], rest[len(sources) :]
        for o in range(total):
            code = code_ref[o]
            which = code // per
            start = pl.multiple_of((code % per) * BLK, BLK)
            for s in range(len(sources)):

                @pl.when(which == s)
                def _(s=s, o=o, start=start):
                    pltpu.make_async_copy(
                        ins[s].at[pl.ds(start, BLK)], buf.at[pl.ds(o * BLK, BLK)], sems.at[o]
                    ).start()

        back = []
        for o in range(total):
            here = pl.ds(o * BLK, BLK)
            pltpu.make_async_copy(ins[0].at[pl.ds(0, BLK)], buf.at[here], sems.at[o]).wait()
            back.append(pltpu.make_async_copy(buf.at[here], out.at[here], osems.at[o]))
            back[-1].start()
        for copy in back:
            copy.wait()

    return call(
        kernel,
        after,
        [codes],
        list(sources),
        [(total * BLK, width)],
        [
            pltpu.VMEM((total * BLK, width), jnp.float32),
            pltpu.SemaphoreType.DMA((total,)),
            pltpu.SemaphoreType.DMA((total,)),
        ],
    )


def assemble(after, front, own, other, tables, first, half_rows):
    rows, width = own.shape
    blocks = rows // BLK

    def kernel(table_ref, front_ref, own_ref, other_ref, out, half, fbuf, abuf, bbuf, sems, osem):
        def copies(o):
            here = pl.ds(o * BLK, BLK)
            a = pl.multiple_of(table_ref[o] * BLK, BLK)
            b = pl.multiple_of(table_ref[blocks + o] * BLK, BLK)
            return (
                pltpu.make_async_copy(
                    front_ref.at[here, pl.ds(first, width)], fbuf.at[here], sems.at[0, o]
                ),
                pltpu.make_async_copy(own_ref.at[pl.ds(a, BLK)], abuf.at[here], sems.at[1, o]),
                pltpu.make_async_copy(other_ref.at[pl.ds(b, BLK)], bbuf.at[here], sems.at[2, o]),
            )

        for o in range(blocks):
            for copy in copies(o):
                copy.start()
        back = []
        for o in range(blocks):
            for copy in copies(o):
                copy.wait()
            here = pl.ds(o * BLK, BLK)
            fbuf[here, :] = (abuf[here, :] + bbuf[here, :]) + fbuf[here, :]
            back.append(pltpu.make_async_copy(fbuf.at[here], out.at[here], sems.at[0, o]))
            back[-1].start()
        mine = pl.multiple_of(table_ref[2 * blocks] * half_rows, BLK)
        last = pltpu.make_async_copy(fbuf.at[pl.ds(mine, half_rows)], half, osem)
        last.start()
        for copy in back:
            copy.wait()
        last.wait()

    return call(
        kernel,
        after,
        [tables],
        [front, own, other],
        [(rows, width), (half_rows, width)],
        [pltpu.VMEM((rows, width), jnp.float32)] * 3
        + [pltpu.SemaphoreType.DMA((3, blocks)), pltpu.SemaphoreType.DMA],
    )


PAIRS = [(0, 1), (0, 2), (1, 0), (1, 2), (2, 0), (2, 1)]
WB = W // BLK


def corner_share(after, child, front, table):
    per = child.shape[0] // BLK
    blocks = NP * WB

    def kernel(table_ref, child_ref, front_ref, out, buf, strip, sem, osem):
        holder = table_ref[2 * blocks] == 1

        def front_copy(n):
            k, c = PAIRS[n]
            return pltpu.make_async_copy(
                front_ref.at[pl.ds(k * W, W), pl.ds(c * W, W)], buf.at[pl.ds(n * W, W)], osem.at[n]
            )

        @pl.when(holder)
        def _():
            for n in range(len(PAIRS)):
                front_copy(n).start()
            for n in range(len(PAIRS)):
                front_copy(n).wait()

        @pl.when(jnp.logical_not(holder))
        def _():
            for n in range(len(PAIRS)):
                buf[n * W : (n + 1) * W, :] = jnp.zeros((W, W), jnp.float32)

        def add_row(p, carry):
            here = table_ref[p]

            @pl.when(here >= 0)
            def _():
                start = pl.multiple_of(here * BLK, BLK)
                copies = []
                for b in range(blocks):
                    source = pl.multiple_of(table_ref[blocks + b] * BLK, BLK)
                    copies.append(
                        pltpu.make_async_copy(
                            child_ref.at[pl.ds(start, BLK), pl.ds(source, BLK)],
                            strip.at[:, pl.ds(b * BLK, BLK)],
                            sem.at[b],
                        )
                    )
                    copies[-1].start()
                for copy in copies:
                    copy.wait()
                k = p // WB
                inner = pl.multiple_of((p % WB) * BLK, BLK)
                for n, (mine, c) in enumerate(PAIRS):

                    @pl.when(k == mine)
                    def _(n=n, c=c):
                        rows = pl.ds(n * W + inner, BLK)
                        buf[rows, :] = buf[rows, :] + strip[:, c * W : (c + 1) * W]

            return carry

        lax.fori_loop(0, blocks, add_row, 0)
        for n in range(len(PAIRS)):
            part = pl.ds(n * W, W)
            pltpu.make_async_copy(buf.at[part], out.at[part], osem.at[n]).start()
        for n in range(len(PAIRS)):
            part = pl.ds(n * W, W)
            pltpu.make_async_copy(buf.at[part], out.at[part], osem.at[n]).wait()

    size = len(PAIRS) * W
    return call(
        kernel,
        after,
        [table],
        [child, front],
        [(size, W)],
        [
            pltpu.VMEM((size, W), jnp.float32),
            pltpu.VMEM((BLK, NP * W), jnp.float32),
            pltpu.SemaphoreType.DMA((blocks,)),
            pltpu.SemaphoreType.DMA((len(PAIRS),)),
        ],
    )


def block_tables(mapping, group):
    total = mapping.shape[0]
    ids = jnp.arange(total, dtype=jnp.int32)
    inverse = jnp.sum(jnp.where(mapping[:, None] == ids[None, :], ids[:, None], 0), axis=0)
    target = mapping // group
    same = (
        (ids[:, None] // group == ids[None, :] // group)
        & (target[:, None] == target[None, :])
        & (ids[None, :] < ids[:, None])
    )
    return inverse, target, jnp.sum(same.astype(jnp.int32), axis=1)


def halves(mine, theirs, sib):
    low = jnp.where(sib == 0, mine, theirs)
    high = jnp.where(sib == 0, theirs, mine)
    return low, high


def local(front, child_updates, child_map, pivot_inverses):
    n_row, n_col = lax.axis_size("row"), lax.axis_size("col")
    row, col, sib = lax.axis_index("row"), lax.axis_index("col"), lax.axis_index("sib")
    rows, cols = front.shape
    child = child_updates[0]
    group, cgroup, per = rows // BLK, cols // BLK, child.shape[0] // BLK
    capacity = group // n_row
    pivots = NP * W
    swap = [(0, 1), (1, 0)]

    inverse, target, rank = block_tables(child_map[0], group)
    shift_to = (col + jnp.arange(n_col, dtype=jnp.int32)) % n_col
    column_table = inverse.reshape(n_col, cgroup)[shift_to].reshape(-1)
    ids = jnp.arange(group, dtype=jnp.int32)
    own = row * group + ids
    slot = target[own] * capacity + rank[own]
    source = jnp.sum(jnp.where(slot[None, :] == ids[:, None], ids[None, :], 0), axis=1)
    codes = (col - source // per) % n_col * per + source % per
    arriving = inverse[own]
    place = arriving // group * capacity + rank[arriving]
    place_other = lax.ppermute(place, "sib", swap)
    place_tables = jnp.concatenate([place, place_other, sib[None].astype(jnp.int32)])

    pivot_ids = jnp.arange(pivots // BLK, dtype=jnp.int32)
    at = inverse[pivot_ids] - (row * n_col + col) * per
    first_device = ((row == 0) & (col == 0) & (sib == 0)).astype(jnp.int32)
    corner_table = jnp.concatenate(
        [
            jnp.where((at >= 0) & (at < per), at, -1),
            inverse[pivot_ids],
            first_device[None],
        ]
    )

    count = len(CHUNKS)
    starts = [sum(CHUNKS[:j]) for j in range(count)]
    widths = [blocks * BLK for blocks in CHUNKS]
    token = jnp.zeros(TOKEN, jnp.float32)
    received, outgoing, A = [], [], []
    ring = [[(i, (i + s) % n_col) for i in range(n_col)] for s in range(n_col)]
    path = [i ^ (i >> 1) for i in range(n_col)]
    along = [(path[i], path[i + 1]) for i in range(n_col - 1)]
    place_on_path = jnp.zeros((), jnp.int32)
    for i, q in enumerate(path):
        place_on_path = place_on_path + jnp.where(col == q, i, 0)
    upward = [(i, i + 1) for i in range(n_row - 1)]
    half_own = rows // 2
    row_ids = row * rows + jnp.arange(rows, dtype=jnp.int32)

    def split(j):
        nonlocal token
        *parts, token = split_columns([token], child, column_table, starts[j], CHUNKS[j], n_col)
        moved = [lax.ppermute(parts[s], "col", ring[s]) for s in range(1, n_col)]
        received.append([parts[0]] + moved)

    def arrange(j):
        nonlocal token
        ordered, token = order_rows([token], received[j], codes)
        mine = lax.all_to_all(
            ordered.reshape(n_row, -1, widths[j]), "row", split_axis=0, concat_axis=0, tiled=True
        ).reshape(rows, widths[j])
        outgoing.append(mine)

    def swap_children(j):
        nonlocal token
        mine, token = hold(token, outgoing[j])
        outgoing[j] = (mine, lax.ppermute(mine, "sib", swap))

    def join(mine):
        low, high = halves(mine, lax.ppermute(mine, "sib", swap), sib)
        return low, high

    panels, rows_held = [], []
    panel_wave, row_wave = [None], [None]
    own_panels = []

    def send_panel(j):
        value = row_wave_panel(j) if j < NP else panel_wave[0]
        if panel_wave[0] is not None and j < NP:
            value = jnp.where(col == 0, value, panel_wave[0])
        panels.append(value)
        panel_wave[0] = lax.ppermute(value, "col", along)

    def row_wave_panel(j):
        work = lax.dynamic_slice_in_dim(A[j], sib * half_own, half_own, 0)
        ids = lax.dynamic_slice_in_dim(row_ids, sib * half_own, half_own, 0)
        for k in range(j):
            masked = jnp.where((ids >= (k + 1) * W)[:, None], own_panels[k], 0.0)
            work = work - dot(masked, corner_upper(k, j), TRAIL)
        own_panels.append(dot(work, pivot_inverses[j], PANEL))
        return own_panels[j]

    def corner_upper(k, j):
        if k == 0:
            return corner[0, j]
        return corner[1, 2] - dot(lower_corner(0, 1), corner[0, 2], TRAIL)

    def lower_corner(k, j):
        if k == 0:
            return dot(corner[j, 0], pivot_inverses[0], PANEL)
        work = corner[2, 1] - dot(lower_corner(0, 2), corner[0, 1], TRAIL)
        return dot(work, pivot_inverses[1], PANEL)

    def send_rows(j, half):
        live = [i for i in range(j - n_row + 1, j + 1) if 0 <= i < count]
        width = max(widths[i] for i in live)
        wave = row_wave[0]
        if half is not None and half.shape[1] < width:
            half = jnp.pad(half, ((0, 0), (0, width - half.shape[1])))
        if wave is not None:
            wave = wave[:, :width]
            if half is not None:
                wave = jnp.where(row == 0, half, wave)
        else:
            wave = half
        rows_held.append(wave)
        live = [i for i in live if i > j - n_row + 1]
        if live:
            width = max(widths[i] for i in live)
            row_wave[0] = lax.ppermute(wave[:, :width], "row", upward)

    def place_blocks(j):
        nonlocal token
        whole, half, token = assemble(
            [token], front, *outgoing[j], place_tables, starts[j] * BLK, pivots // 2
        )
        A.append(whole)
        send_rows(j, half)
        if j < NP + n_col - 2:
            send_panel(j)

    split(0)
    share, token = corner_share([token], child, front, corner_table)
    share = lax.psum(share, ("sib", "row", "col"))
    corner = {pair: share[n * W : (n + 1) * W] for n, pair in enumerate(PAIRS)}
    split(1)
    arrange(0)
    split(2)
    arrange(1)
    swap_children(0)
    for j in range(count):
        if j + 3 < count:
            split(j + 3)
        if j + 2 < count:
            arrange(j + 2)
        place_blocks(j)
        if j + 1 < count:
            swap_children(j + 1)
    panels.append(panel_wave[0])
    for j in range(count, count + n_row - 1):
        send_rows(j, None)

    def pick(held, where_here, steps, width):
        value = held[0][:, :width]
        for i in range(1, steps):
            value = jnp.where(where_here == i, held[i][:, :width], value)
        return value

    lower, final = [], []
    for k in range(NP):
        low, high = join(pick(panels[k:], place_on_path, n_col, W))
        final.append(jnp.concatenate([low, high], axis=0))
        lower.append(jnp.where((row_ids >= (k + 1) * W)[:, None], final[k], 0.0))
    below = {(k, c): lower_corner(k, c) for k in range(NP) for c in range(k + 1, NP)}

    outs = []
    for j in range(count):
        low, high = join(pick(rows_held[j:], row, n_row, widths[j]))
        raw = jnp.concatenate([low, high], axis=0)
        R = [raw[k * W : (k + 1) * W] for k in range(NP)]
        for k in range(NP):
            for later in range(k + 1, NP):
                R[later] = R[later] - dot(below[k, later], R[k], TRAIL)
        value = A[j]
        for some in (range(NP - 1), range(NP - 1, NP)):
            value = value - dot(
                jnp.concatenate([lower[k] for k in some], axis=1),
                jnp.concatenate([R[k] for k in some], axis=0),
                TRAIL,
            )
        outs.append(jnp.where(col == 0, final[j], value) if j < NP else value)
    return jnp.concatenate(outs, axis=1)


def spread(value, axis, source):
    kept = jnp.where(lax.axis_index(axis) == source, value, 0).astype(value.dtype)
    return lax.psum(kept, axis)


def plain_local(front, child_updates, child_map, pivot_inverses):
    row_count = lax.axis_size("row")
    row_here = lax.axis_index("row")
    col_here = lax.axis_index("col")
    sib_here = lax.axis_index("sib")
    rows_dev, cols_dev = front.shape
    group_blocks = rows_dev // BLK
    total_blocks = child_map.shape[1]
    capacity = max(1, group_blocks * group_blocks // total_blocks)
    inverse_map, target_group, rank_of = block_tables(child_map[0], group_blocks)
    columns = jnp.arange(F, dtype=jnp.int32)
    column_source = inverse_map[columns // BLK] * BLK + columns % BLK
    permuted = jnp.take(child_updates[0], column_source, axis=1)
    group_rows = lax.all_to_all(permuted, "col", split_axis=1, concat_axis=0, tiled=True)
    local_blocks = group_rows.reshape(group_blocks, BLK, cols_dev)
    local_ids = jnp.arange(group_blocks, dtype=jnp.int32)
    own_blocks = row_here * group_blocks + local_ids
    send_slot = target_group[own_blocks] * capacity + rank_of[own_blocks]
    slot_ids = jnp.arange(row_count * capacity, dtype=jnp.int32)
    slot_hits = send_slot[None, :] == slot_ids[:, None]
    source_block = jnp.sum(jnp.where(slot_hits, local_ids[None, :], 0), axis=1)
    filled = jnp.any(slot_hits, axis=1)
    outgoing = jnp.where(filled[:, None, None], jnp.take(local_blocks, source_block, axis=0), 0.0)
    incoming = lax.all_to_all(
        outgoing.reshape(row_count * capacity * BLK, cols_dev),
        "row",
        split_axis=0,
        concat_axis=0,
        tiled=True,
    )
    arriving = inverse_map[own_blocks]
    receive_slot = arriving // group_blocks * capacity + rank_of[arriving]
    relocated = jnp.take(
        incoming.reshape(row_count * capacity, BLK, cols_dev), receive_slot, axis=0
    ).reshape(rows_dev, cols_dev)
    half_rows = rows_dev // 2
    working = lax.psum_scatter(
        relocated, "sib", scatter_dimension=0, tiled=True
    ) + lax.dynamic_slice_in_dim(front, sib_here * half_rows, half_rows, 0)
    row_start = row_here * rows_dev + sib_here * half_rows
    global_rows = row_start + jnp.arange(working.shape[0], dtype=jnp.int32)
    global_cols = col_here * cols_dev + jnp.arange(cols_dev, dtype=jnp.int32)
    for panel_index in range(NP):
        first_col = panel_index * W
        after_panel = first_col + W
        col_root = first_col // cols_dev
        col_offset = first_col % cols_dev
        pivot_cols = working[:, col_offset : col_offset + W]
        pivot_cols = spread(pivot_cols, "col", col_root)
        group_offset = first_col % rows_dev
        row_root = group_offset // half_rows * row_count + first_col // rows_dev
        row_offset = group_offset % half_rows
        pivot_rows = spread(working[row_offset : row_offset + W, :], ("sib", "row"), row_root)
        panel_block = jnp.dot(
            pivot_cols,
            pivot_inverses[panel_index],
            precision=lax.Precision.HIGHEST,
            preferred_element_type=jnp.float32,
        )
        update = jnp.dot(
            panel_block,
            pivot_rows,
            precision=lax.Precision.HIGHEST,
            preferred_element_type=jnp.float32,
        )
        inside = (global_rows >= after_panel)[:, None] & (global_cols >= after_panel)[None, :]
        working = working - jnp.where(inside, update, 0.0)
        placed = lax.dynamic_update_slice(working, panel_block, (0, col_offset))
        working = jnp.where(col_here == col_root, placed, working)
    working = lax.all_gather(working, "sib", axis=0, tiled=True)
    return working

def solution(mesh):
    placed = (P("row", "col"), P("sib", ("row", "col"), None), P("sib", None), P())
    rows, cols = F // mesh.shape["row"], F // mesh.shape["col"]
    wide = rows >= NP * W and cols == sum(CHUNKS) * BLK and mesh.shape["sib"] == 2
    return jax.shard_map(
        local if wide else plain_local,
        mesh=mesh,
        in_specs=placed,
        out_specs=P("row", "col"),
        check_vma=False,
    )
```

```python
import jax
import jax.numpy as jnp
from jax import lax
from jax.experimental import pallas as pl
from jax.experimental.pallas import tpu as pltpu
from jax.sharding import PartitionSpec as P

F = 8192
W = 512
BLK = 128
NP = 3
CHUNKS = (4, 4, 4, 2, 2)
VMEM_LIMIT = 48 * 1024 * 1024
TRAIL = lax.Precision.HIGH
PANEL = lax.Precision.HIGHEST


def dot(a, b, precision):
    return jnp.dot(a, b, precision=precision, preferred_element_type=jnp.float32)


TOKEN = (8, 128)


def call(kernel, after, tables, arrays, outs, scratch):
    def ordered(*refs):
        n = len(tables) + len(arrays)
        m = n + len(after)
        kernel(*refs[:n], *refs[m : m + len(outs)], *refs[m + 1 + len(outs) :])

    return pl.pallas_call(
        ordered,
        out_shape=[jax.ShapeDtypeStruct(shape, jnp.float32) for shape in (*outs, TOKEN)],
        in_specs=[pl.BlockSpec(memory_space=pltpu.SMEM)] * len(tables)
        + [pl.BlockSpec(memory_space=pl.ANY)] * (len(arrays) + len(after)),
        out_specs=[pl.BlockSpec(memory_space=pl.ANY)] * (len(outs) + 1),
        scratch_shapes=scratch,
        compiler_params=pltpu.CompilerParams(vmem_limit_bytes=VMEM_LIMIT),
        cost_estimate=pl.CostEstimate(flops=0, bytes_accessed=4096, transcendentals=0),
    )(*tables, *arrays, *after)


def hold(after, value):
    def kernel(*refs):
        pass

    return pl.pallas_call(
        kernel,
        out_shape=[
            jax.ShapeDtypeStruct(value.shape, jnp.float32),
            jax.ShapeDtypeStruct(TOKEN, jnp.float32),
        ],
        in_specs=[pl.BlockSpec(memory_space=pl.ANY)] * (1 + len(after)),
        out_specs=[pl.BlockSpec(memory_space=pl.ANY)] * 2,
        input_output_aliases={0: 0},
        cost_estimate=pl.CostEstimate(flops=0, bytes_accessed=4096, transcendentals=0),
    )(value, *after)


def split_columns(after, child, table, first, count, parts):
    rows = child.shape[0]
    stride = table.shape[0] // parts

    def kernel(table_ref, child_ref, *rest):
        outs, (buf, sems, osems) = rest[:parts], rest[parts:]
        into, back = [], []
        for part in range(parts):
            for b in range(count):
                source = pl.multiple_of(table_ref[part * stride + first + b] * BLK, BLK)
                into.append(
                    pltpu.make_async_copy(
                        child_ref.at[:, pl.ds(source, BLK)],
                        buf.at[part, :, pl.ds(b * BLK, BLK)],
                        sems.at[part * count + b],
                    )
                )
                into[-1].start()
        for part in range(parts):
            for b in range(count):
                into[part * count + b].wait()
            back.append(pltpu.make_async_copy(buf.at[part], outs[part], osems.at[part]))
            back[-1].start()
        for copy in back:
            copy.wait()

    return call(
        kernel,
        after,
        [table],
        [child],
        [(rows, count * BLK)] * parts,
        [
            pltpu.VMEM((parts, rows, count * BLK), jnp.float32),
            pltpu.SemaphoreType.DMA((parts * count,)),
            pltpu.SemaphoreType.DMA((parts,)),
        ],
    )


def order_rows(after, sources, codes):
    rows, width = sources[0].shape
    per = rows // BLK
    total = codes.shape[0]

    def kernel(code_ref, *rest):
        ins, (out, buf, sems, osems) = rest[: len(sources)], rest[len(sources) :]
        for o in range(total):
            code = code_ref[o]
            which = code // per
            start = pl.multiple_of((code % per) * BLK, BLK)
            for s in range(len(sources)):

                @pl.when(which == s)
                def _(s=s, o=o, start=start):
                    pltpu.make_async_copy(
                        ins[s].at[pl.ds(start, BLK)], buf.at[pl.ds(o * BLK, BLK)], sems.at[o]
                    ).start()

        back = []
        for o in range(total):
            here = pl.ds(o * BLK, BLK)
            pltpu.make_async_copy(ins[0].at[pl.ds(0, BLK)], buf.at[here], sems.at[o]).wait()
            back.append(pltpu.make_async_copy(buf.at[here], out.at[here], osems.at[o]))
            back[-1].start()
        for copy in back:
            copy.wait()

    return call(
        kernel,
        after,
        [codes],
        list(sources),
        [(total * BLK, width)],
        [
            pltpu.VMEM((total * BLK, width), jnp.float32),
            pltpu.SemaphoreType.DMA((total,)),
            pltpu.SemaphoreType.DMA((total,)),
        ],
    )


def assemble(after, front, own, other, tables, first, half_rows):
    rows, width = own.shape
    blocks = rows // BLK

    def kernel(table_ref, front_ref, own_ref, other_ref, out, half, fbuf, abuf, bbuf, sems, osem):
        def copies(o):
            here = pl.ds(o * BLK, BLK)
            a = pl.multiple_of(table_ref[o] * BLK, BLK)
            b = pl.multiple_of(table_ref[blocks + o] * BLK, BLK)
            return (
                pltpu.make_async_copy(
                    front_ref.at[here, pl.ds(first, width)], fbuf.at[here], sems.at[0, o]
                ),
                pltpu.make_async_copy(own_ref.at[pl.ds(a, BLK)], abuf.at[here], sems.at[1, o]),
                pltpu.make_async_copy(other_ref.at[pl.ds(b, BLK)], bbuf.at[here], sems.at[2, o]),
            )

        for o in range(blocks):
            for copy in copies(o):
                copy.start()
        back = []
        for o in range(blocks):
            for copy in copies(o):
                copy.wait()
            here = pl.ds(o * BLK, BLK)
            fbuf[here, :] = (abuf[here, :] + bbuf[here, :]) + fbuf[here, :]
            back.append(pltpu.make_async_copy(fbuf.at[here], out.at[here], sems.at[0, o]))
            back[-1].start()
        mine = pl.multiple_of(table_ref[2 * blocks] * half_rows, BLK)
        last = pltpu.make_async_copy(fbuf.at[pl.ds(mine, half_rows)], half, osem)
        last.start()
        for copy in back:
            copy.wait()
        last.wait()

    return call(
        kernel,
        after,
        [tables],
        [front, own, other],
        [(rows, width), (half_rows, width)],
        [pltpu.VMEM((rows, width), jnp.float32)] * 3
        + [pltpu.SemaphoreType.DMA((3, blocks)), pltpu.SemaphoreType.DMA],
    )


PAIRS = [(0, 1), (0, 2), (1, 0), (1, 2), (2, 0), (2, 1)]
WB = W // BLK


def corner_share(after, child, front, table):
    per = child.shape[0] // BLK
    blocks = NP * WB

    def kernel(table_ref, child_ref, front_ref, out, buf, strip, sem, osem):
        holder = table_ref[2 * blocks] == 1

        def front_copy(n):
            k, c = PAIRS[n]
            return pltpu.make_async_copy(
                front_ref.at[pl.ds(k * W, W), pl.ds(c * W, W)], buf.at[pl.ds(n * W, W)], osem.at[n]
            )

        @pl.when(holder)
        def _():
            for n in range(len(PAIRS)):
                front_copy(n).start()
            for n in range(len(PAIRS)):
                front_copy(n).wait()

        @pl.when(jnp.logical_not(holder))
        def _():
            for n in range(len(PAIRS)):
                buf[n * W : (n + 1) * W, :] = jnp.zeros((W, W), jnp.float32)

        def add_row(p, carry):
            here = table_ref[p]

            @pl.when(here >= 0)
            def _():
                start = pl.multiple_of(here * BLK, BLK)
                copies = []
                for b in range(blocks):
                    source = pl.multiple_of(table_ref[blocks + b] * BLK, BLK)
                    copies.append(
                        pltpu.make_async_copy(
                            child_ref.at[pl.ds(start, BLK), pl.ds(source, BLK)],
                            strip.at[:, pl.ds(b * BLK, BLK)],
                            sem.at[b],
                        )
                    )
                    copies[-1].start()
                for copy in copies:
                    copy.wait()
                k = p // WB
                inner = pl.multiple_of((p % WB) * BLK, BLK)
                for n, (mine, c) in enumerate(PAIRS):

                    @pl.when(k == mine)
                    def _(n=n, c=c):
                        rows = pl.ds(n * W + inner, BLK)
                        buf[rows, :] = buf[rows, :] + strip[:, c * W : (c + 1) * W]

            return carry

        lax.fori_loop(0, blocks, add_row, 0)
        for n in range(len(PAIRS)):
            part = pl.ds(n * W, W)
            pltpu.make_async_copy(buf.at[part], out.at[part], osem.at[n]).start()
        for n in range(len(PAIRS)):
            part = pl.ds(n * W, W)
            pltpu.make_async_copy(buf.at[part], out.at[part], osem.at[n]).wait()

    size = len(PAIRS) * W
    return call(
        kernel,
        after,
        [table],
        [child, front],
        [(size, W)],
        [
            pltpu.VMEM((size, W), jnp.float32),
            pltpu.VMEM((BLK, NP * W), jnp.float32),
            pltpu.SemaphoreType.DMA((blocks,)),
            pltpu.SemaphoreType.DMA((len(PAIRS),)),
        ],
    )


def block_tables(mapping, group):
    total = mapping.shape[0]
    ids = jnp.arange(total, dtype=jnp.int32)
    inverse = jnp.sum(jnp.where(mapping[:, None] == ids[None, :], ids[:, None], 0), axis=0)
    target = mapping // group
    same = (
        (ids[:, None] // group == ids[None, :] // group)
        & (target[:, None] == target[None, :])
        & (ids[None, :] < ids[:, None])
    )
    return inverse, target, jnp.sum(same.astype(jnp.int32), axis=1)


def halves(mine, theirs, sib):
    low = jnp.where(sib == 0, mine, theirs)
    high = jnp.where(sib == 0, theirs, mine)
    return low, high


def local(front, child_updates, child_map, pivot_inverses):
    n_row, n_col = lax.axis_size("row"), lax.axis_size("col")
    row, col, sib = lax.axis_index("row"), lax.axis_index("col"), lax.axis_index("sib")
    rows, cols = front.shape
    child = child_updates[0]
    group, cgroup, per = rows // BLK, cols // BLK, child.shape[0] // BLK
    capacity = group // n_row
    pivots = NP * W
    swap = [(0, 1), (1, 0)]

    inverse, target, rank = block_tables(child_map[0], group)
    shift_to = (col + jnp.arange(n_col, dtype=jnp.int32)) % n_col
    column_table = inverse.reshape(n_col, cgroup)[shift_to].reshape(-1)
    ids = jnp.arange(group, dtype=jnp.int32)
    own = row * group + ids
    slot = target[own] * capacity + rank[own]
    source = jnp.sum(jnp.where(slot[None, :] == ids[:, None], ids[None, :], 0), axis=1)
    codes = (col - source // per) % n_col * per + source % per
    arriving = inverse[own]
    place = arriving // group * capacity + rank[arriving]
    place_other = lax.ppermute(place, "sib", swap)
    place_tables = jnp.concatenate([place, place_other, sib[None].astype(jnp.int32)])

    pivot_ids = jnp.arange(pivots // BLK, dtype=jnp.int32)
    at = inverse[pivot_ids] - (row * n_col + col) * per
    first_device = ((row == 0) & (col == 0) & (sib == 0)).astype(jnp.int32)
    corner_table = jnp.concatenate(
        [
            jnp.where((at >= 0) & (at < per), at, -1),
            inverse[pivot_ids],
            first_device[None],
        ]
    )

    count = len(CHUNKS)
    starts = [sum(CHUNKS[:j]) for j in range(count)]
    widths = [blocks * BLK for blocks in CHUNKS]
    token = jnp.zeros(TOKEN, jnp.float32)
    received, outgoing, A = [], [], []
    ring = [[(i, (i + s) % n_col) for i in range(n_col)] for s in range(n_col)]
    bits = n_col.bit_length() - 1
    path = [i ^ (i >> 1) for i in range(n_col)]
    mirror = [sum((q >> b & 1) << bits - 1 - b for b in range(bits)) for q in path]
    along, place_on_path = [], jnp.zeros((), jnp.int32)
    for core, way in enumerate((path, mirror)):
        along += [(core * n_col + way[i], core * n_col + way[i + 1]) for i in range(n_col - 1)]
        for i, q in enumerate(way):
            place_on_path = place_on_path + jnp.where((sib == core) & (col == q), i, 0)
    upward = [(i, i + 1) for i in range(n_row - 1)]
    half_own = rows // 2
    row_ids = row * rows + jnp.arange(rows, dtype=jnp.int32)

    def split(j):
        nonlocal token
        *parts, token = split_columns([token], child, column_table, starts[j], CHUNKS[j], n_col)
        moved = [lax.ppermute(parts[s], "col", ring[s]) for s in range(1, n_col)]
        received.append([parts[0]] + moved)

    def arrange(j):
        nonlocal token
        ordered, token = order_rows([token], received[j], codes)
        mine = lax.all_to_all(
            ordered.reshape(n_row, -1, widths[j]), "row", split_axis=0, concat_axis=0, tiled=True
        ).reshape(rows, widths[j])
        outgoing.append(mine)

    def swap_children(j):
        nonlocal token
        waits = row_waits[-1:] + panel_waits[j - 3 : j - 2 if j > 2 else 0]
        if row_wave[0] is not None:
            row_waits.append(row_wave[0])
            panel_waits.append(panel_wave[0])
        mine, token = hold([token, *waits], outgoing[j])
        outgoing[j] = (mine, lax.ppermute(mine, "sib", swap))

    def join(mine):
        low, high = halves(mine, lax.ppermute(mine, "sib", swap), sib)
        return low, high

    panels, rows_held = [], []
    panel_wave, row_wave, row_waits, panel_waits = [None], [None], [], []
    own_panels = []

    def send_panel(j):
        value = row_wave_panel(j) if j < NP else panel_wave[0]
        if panel_wave[0] is not None and j < NP:
            value = jnp.where(col == 0, value, panel_wave[0])
        panels.append(value)
        panel_wave[0] = lax.ppermute(value, ("sib", "col"), along)

    def row_wave_panel(j):
        work = lax.dynamic_slice_in_dim(A[j], sib * half_own, half_own, 0)
        ids = lax.dynamic_slice_in_dim(row_ids, sib * half_own, half_own, 0)
        for k in range(j):
            masked = jnp.where((ids >= (k + 1) * W)[:, None], own_panels[k], 0.0)
            work = work - dot(masked, corner_upper(k, j), TRAIL)
        own_panels.append(dot(work, pivot_inverses[j], PANEL))
        return own_panels[j]

    def corner_upper(k, j):
        if k == 0:
            return corner[0, j]
        return corner[1, 2] - dot(lower_corner(0, 1), corner[0, 2], TRAIL)

    def lower_corner(k, j):
        if k == 0:
            return dot(corner[j, 0], pivot_inverses[0], PANEL)
        work = corner[2, 1] - dot(lower_corner(0, 2), corner[0, 1], TRAIL)
        return dot(work, pivot_inverses[1], PANEL)

    def send_rows(j, half):
        live = [i for i in range(j - n_row + 1, j + 1) if 0 <= i < count]
        width = max(widths[i] for i in live)
        wave = row_wave[0]
        if half is not None and half.shape[1] < width:
            half = jnp.pad(half, ((0, 0), (0, width - half.shape[1])))
        if wave is not None:
            wave = wave[:, :width]
            if half is not None:
                wave = jnp.where(row == 0, half, wave)
        else:
            wave = half
        rows_held.append(wave)
        live = [i for i in live if i > j - n_row + 1]
        if live:
            width = max(widths[i] for i in live)
            row_wave[0] = lax.ppermute(wave[:, :width], "row", upward)

    def place_blocks(j):
        nonlocal token
        whole, half, token = assemble(
            [token], front, *outgoing[j], place_tables, starts[j] * BLK, pivots // 2
        )
        A.append(whole)
        send_rows(j, half)
        if j < NP + n_col - 2:
            send_panel(j)

    split(0)
    share, token = corner_share([token], child, front, corner_table)
    everywhere = ("sib", "row", "col")
    share = lax.psum_scatter(share, everywhere, scatter_dimension=0, tiled=True)
    share = lax.all_gather(share, everywhere, axis=0, tiled=True)
    corner = {pair: share[n * W : (n + 1) * W] for n, pair in enumerate(PAIRS)}
    split(1)
    arrange(0)
    split(2)
    arrange(1)
    swap_children(0)
    for j in range(count):
        if j + 3 < count:
            split(j + 3)
        if j + 2 < count:
            arrange(j + 2)
        place_blocks(j)
        if j + 1 < count:
            swap_children(j + 1)
    panels.append(panel_wave[0])
    for j in range(count, count + n_row - 1):
        send_rows(j, None)

    def pick(held, where_here, steps, width):
        value = held[0][:, :width]
        for i in range(1, steps):
            value = jnp.where(where_here == i, held[i][:, :width], value)
        return value

    half_ids = lax.dynamic_slice_in_dim(row_ids, sib * half_own, half_own, 0)
    lower, final = [], []
    for k in range(NP):
        final.append(pick(panels[k:], place_on_path, n_col, W))
        lower.append(jnp.where((half_ids >= (k + 1) * W)[:, None], final[k], 0.0))
    below = {(k, c): lower_corner(k, c) for k in range(NP) for c in range(k + 1, NP)}

    outs = []
    for j in range(count):
        low, high = join(pick(rows_held[j:], row, n_row, widths[j]))
        raw = jnp.concatenate([low, high], axis=0)
        R = [raw[k * W : (k + 1) * W] for k in range(NP)]
        for k in range(NP):
            for later in range(k + 1, NP):
                R[later] = R[later] - dot(below[k, later], R[k], TRAIL)
        value = lax.dynamic_slice_in_dim(A[j], sib * half_own, half_own, 0)
        value = value - dot(jnp.concatenate(lower, axis=1), jnp.concatenate(R, axis=0), TRAIL)
        if j < NP:
            value = jnp.where(col == 0, final[j], value)
        outs.append(jnp.concatenate(join(value), axis=0))
    return jnp.concatenate(outs, axis=1)


def spread(value, axis, source):
    kept = jnp.where(lax.axis_index(axis) == source, value, 0).astype(value.dtype)
    return lax.psum(kept, axis)


def plain_local(front, child_updates, child_map, pivot_inverses):
    row_count = lax.axis_size("row")
    row_here = lax.axis_index("row")
    col_here = lax.axis_index("col")
    sib_here = lax.axis_index("sib")
    rows_dev, cols_dev = front.shape
    group_blocks = rows_dev // BLK
    total_blocks = child_map.shape[1]
    capacity = max(1, group_blocks * group_blocks // total_blocks)
    inverse_map, target_group, rank_of = block_tables(child_map[0], group_blocks)
    columns = jnp.arange(F, dtype=jnp.int32)
    column_source = inverse_map[columns // BLK] * BLK + columns % BLK
    permuted = jnp.take(child_updates[0], column_source, axis=1)
    group_rows = lax.all_to_all(permuted, "col", split_axis=1, concat_axis=0, tiled=True)
    local_blocks = group_rows.reshape(group_blocks, BLK, cols_dev)
    local_ids = jnp.arange(group_blocks, dtype=jnp.int32)
    own_blocks = row_here * group_blocks + local_ids
    send_slot = target_group[own_blocks] * capacity + rank_of[own_blocks]
    slot_ids = jnp.arange(row_count * capacity, dtype=jnp.int32)
    slot_hits = send_slot[None, :] == slot_ids[:, None]
    source_block = jnp.sum(jnp.where(slot_hits, local_ids[None, :], 0), axis=1)
    filled = jnp.any(slot_hits, axis=1)
    outgoing = jnp.where(filled[:, None, None], jnp.take(local_blocks, source_block, axis=0), 0.0)
    incoming = lax.all_to_all(
        outgoing.reshape(row_count * capacity * BLK, cols_dev),
        "row",
        split_axis=0,
        concat_axis=0,
        tiled=True,
    )
    arriving = inverse_map[own_blocks]
    receive_slot = arriving // group_blocks * capacity + rank_of[arriving]
    relocated = jnp.take(
        incoming.reshape(row_count * capacity, BLK, cols_dev), receive_slot, axis=0
    ).reshape(rows_dev, cols_dev)
    half_rows = rows_dev // 2
    working = lax.psum_scatter(
        relocated, "sib", scatter_dimension=0, tiled=True
    ) + lax.dynamic_slice_in_dim(front, sib_here * half_rows, half_rows, 0)
    row_start = row_here * rows_dev + sib_here * half_rows
    global_rows = row_start + jnp.arange(working.shape[0], dtype=jnp.int32)
    global_cols = col_here * cols_dev + jnp.arange(cols_dev, dtype=jnp.int32)
    for panel_index in range(NP):
        first_col = panel_index * W
        after_panel = first_col + W
        col_root = first_col // cols_dev
        col_offset = first_col % cols_dev
        pivot_cols = working[:, col_offset : col_offset + W]
        pivot_cols = spread(pivot_cols, "col", col_root)
        group_offset = first_col % rows_dev
        row_root = group_offset // half_rows * row_count + first_col // rows_dev
        row_offset = group_offset % half_rows
        pivot_rows = spread(working[row_offset : row_offset + W, :], ("sib", "row"), row_root)
        panel_block = jnp.dot(
            pivot_cols,
            pivot_inverses[panel_index],
            precision=lax.Precision.HIGHEST,
            preferred_element_type=jnp.float32,
        )
        update = jnp.dot(
            panel_block,
            pivot_rows,
            precision=lax.Precision.HIGHEST,
            preferred_element_type=jnp.float32,
        )
        inside = (global_rows >= after_panel)[:, None] & (global_cols >= after_panel)[None, :]
        working = working - jnp.where(inside, update, 0.0)
        placed = lax.dynamic_update_slice(working, panel_block, (0, col_offset))
        working = jnp.where(col_here == col_root, placed, working)
    working = lax.all_gather(working, "sib", axis=0, tiled=True)
    return working

def solution(mesh):
    placed = (P("row", "col"), P("sib", ("row", "col"), None), P("sib", None), P())
    rows, cols = F // mesh.shape["row"], F // mesh.shape["col"]
    wide = rows >= NP * W and cols == sum(CHUNKS) * BLK and mesh.shape["sib"] == 2
    return jax.shard_map(
        local if wide else plain_local,
        mesh=mesh,
        in_specs=placed,
        out_specs=P("row", "col"),
        check_vma=False,
    )
```

```python
import jax
import jax.numpy as jnp
from jax import lax
from jax.experimental import pallas as pl
from jax.experimental.pallas import tpu as pltpu
from jax.sharding import PartitionSpec as P

F = 8192
W = 512
BLK = 128
NP = 3
CHUNKS = (4, 4, 4, 2, 2)
VMEM_LIMIT = 48 * 1024 * 1024
TRAIL = lax.Precision.HIGH
PANEL = lax.Precision.HIGHEST


def dot(a, b, precision):
    return jnp.dot(a, b, precision=precision, preferred_element_type=jnp.float32)


TOKEN = (8, 128)


def call(kernel, after, tables, arrays, outs, scratch):
    def ordered(*refs):
        n = len(tables) + len(arrays)
        m = n + len(after)
        kernel(*refs[:n], *refs[m : m + len(outs)], *refs[m + 1 + len(outs) :])

    return pl.pallas_call(
        ordered,
        out_shape=[jax.ShapeDtypeStruct(shape, jnp.float32) for shape in (*outs, TOKEN)],
        in_specs=[pl.BlockSpec(memory_space=pltpu.SMEM)] * len(tables)
        + [pl.BlockSpec(memory_space=pl.ANY)] * (len(arrays) + len(after)),
        out_specs=[pl.BlockSpec(memory_space=pl.ANY)] * (len(outs) + 1),
        scratch_shapes=scratch,
        compiler_params=pltpu.CompilerParams(vmem_limit_bytes=VMEM_LIMIT),
        cost_estimate=pl.CostEstimate(flops=0, bytes_accessed=4096, transcendentals=0),
    )(*tables, *arrays, *after)


def hold(after, value):
    def kernel(*refs):
        pass

    return pl.pallas_call(
        kernel,
        out_shape=[
            jax.ShapeDtypeStruct(value.shape, jnp.float32),
            jax.ShapeDtypeStruct(TOKEN, jnp.float32),
        ],
        in_specs=[pl.BlockSpec(memory_space=pl.ANY)] * (1 + len(after)),
        out_specs=[pl.BlockSpec(memory_space=pl.ANY)] * 2,
        input_output_aliases={0: 0},
        cost_estimate=pl.CostEstimate(flops=0, bytes_accessed=4096, transcendentals=0),
    )(value, *after)


def split_columns(after, child, table, first, count, parts):
    rows = child.shape[0]
    stride = table.shape[0] // parts

    def kernel(table_ref, child_ref, *rest):
        outs, (buf, sems, osems) = rest[:parts], rest[parts:]
        into, back = [], []
        for part in range(parts):
            for b in range(count):
                source = pl.multiple_of(table_ref[part * stride + first + b] * BLK, BLK)
                into.append(
                    pltpu.make_async_copy(
                        child_ref.at[:, pl.ds(source, BLK)],
                        buf.at[part, :, pl.ds(b * BLK, BLK)],
                        sems.at[part * count + b],
                    )
                )
                into[-1].start()
        for part in range(parts):
            for b in range(count):
                into[part * count + b].wait()
            back.append(pltpu.make_async_copy(buf.at[part], outs[part], osems.at[part]))
            back[-1].start()
        for copy in back:
            copy.wait()

    return call(
        kernel,
        after,
        [table],
        [child],
        [(rows, count * BLK)] * parts,
        [
            pltpu.VMEM((parts, rows, count * BLK), jnp.float32),
            pltpu.SemaphoreType.DMA((parts * count,)),
            pltpu.SemaphoreType.DMA((parts,)),
        ],
    )


def order_rows(after, sources, codes):
    rows, width = sources[0].shape
    per = rows // BLK
    total = codes.shape[0]

    def kernel(code_ref, *rest):
        ins, (out, buf, sems, osems) = rest[: len(sources)], rest[len(sources) :]
        for o in range(total):
            code = code_ref[o]
            which = code // per
            start = pl.multiple_of((code % per) * BLK, BLK)
            for s in range(len(sources)):

                @pl.when(which == s)
                def _(s=s, o=o, start=start):
                    pltpu.make_async_copy(
                        ins[s].at[pl.ds(start, BLK)], buf.at[pl.ds(o * BLK, BLK)], sems.at[o]
                    ).start()

        back = []
        for o in range(total):
            here = pl.ds(o * BLK, BLK)
            pltpu.make_async_copy(ins[0].at[pl.ds(0, BLK)], buf.at[here], sems.at[o]).wait()
            back.append(pltpu.make_async_copy(buf.at[here], out.at[here], osems.at[o]))
            back[-1].start()
        for copy in back:
            copy.wait()

    return call(
        kernel,
        after,
        [codes],
        list(sources),
        [(total * BLK, width)],
        [
            pltpu.VMEM((total * BLK, width), jnp.float32),
            pltpu.SemaphoreType.DMA((total,)),
            pltpu.SemaphoreType.DMA((total,)),
        ],
    )


def assemble(after, front, own, other, tables, first, half_rows):
    rows, width = own.shape
    blocks = rows // BLK

    def kernel(table_ref, front_ref, own_ref, other_ref, out, half, fbuf, abuf, bbuf, sems, osem):
        def copies(o):
            here = pl.ds(o * BLK, BLK)
            a = pl.multiple_of(table_ref[o] * BLK, BLK)
            b = pl.multiple_of(table_ref[blocks + o] * BLK, BLK)
            return (
                pltpu.make_async_copy(
                    front_ref.at[here, pl.ds(first, width)], fbuf.at[here], sems.at[0, o]
                ),
                pltpu.make_async_copy(own_ref.at[pl.ds(a, BLK)], abuf.at[here], sems.at[1, o]),
                pltpu.make_async_copy(other_ref.at[pl.ds(b, BLK)], bbuf.at[here], sems.at[2, o]),
            )

        for o in range(blocks):
            for copy in copies(o):
                copy.start()
        back = []
        for o in range(blocks):
            for copy in copies(o):
                copy.wait()
            here = pl.ds(o * BLK, BLK)
            fbuf[here, :] = (abuf[here, :] + bbuf[here, :]) + fbuf[here, :]
            back.append(pltpu.make_async_copy(fbuf.at[here], out.at[here], sems.at[0, o]))
            back[-1].start()
        mine = pl.multiple_of(table_ref[2 * blocks] * half_rows, BLK)
        last = pltpu.make_async_copy(fbuf.at[pl.ds(mine, half_rows)], half, osem)
        last.start()
        for copy in back:
            copy.wait()
        last.wait()

    return call(
        kernel,
        after,
        [tables],
        [front, own, other],
        [(rows, width), (half_rows, width)],
        [pltpu.VMEM((rows, width), jnp.float32)] * 3
        + [pltpu.SemaphoreType.DMA((3, blocks)), pltpu.SemaphoreType.DMA],
    )


PAIRS = [(0, 1), (0, 2), (1, 0), (1, 2), (2, 0), (2, 1)]
WB = W // BLK


def corner_share(after, child, front, table):
    per = child.shape[0] // BLK
    blocks = NP * WB

    def kernel(table_ref, child_ref, front_ref, out, buf, strip, sem, osem):
        holder = table_ref[2 * blocks] == 1

        def front_copy(n):
            k, c = PAIRS[n]
            return pltpu.make_async_copy(
                front_ref.at[pl.ds(k * W, W), pl.ds(c * W, W)], buf.at[pl.ds(n * W, W)], osem.at[n]
            )

        @pl.when(holder)
        def _():
            for n in range(len(PAIRS)):
                front_copy(n).start()
            for n in range(len(PAIRS)):
                front_copy(n).wait()

        @pl.when(jnp.logical_not(holder))
        def _():
            for n in range(len(PAIRS)):
                buf[n * W : (n + 1) * W, :] = jnp.zeros((W, W), jnp.float32)

        def add_row(p, carry):
            here = table_ref[p]

            @pl.when(here >= 0)
            def _():
                start = pl.multiple_of(here * BLK, BLK)
                copies = []
                for b in range(blocks):
                    source = pl.multiple_of(table_ref[blocks + b] * BLK, BLK)
                    copies.append(
                        pltpu.make_async_copy(
                            child_ref.at[pl.ds(start, BLK), pl.ds(source, BLK)],
                            strip.at[:, pl.ds(b * BLK, BLK)],
                            sem.at[b],
                        )
                    )
                    copies[-1].start()
                for copy in copies:
                    copy.wait()
                k = p // WB
                inner = pl.multiple_of((p % WB) * BLK, BLK)
                for n, (mine, c) in enumerate(PAIRS):

                    @pl.when(k == mine)
                    def _(n=n, c=c):
                        rows = pl.ds(n * W + inner, BLK)
                        buf[rows, :] = buf[rows, :] + strip[:, c * W : (c + 1) * W]

            return carry

        lax.fori_loop(0, blocks, add_row, 0)
        for n in range(len(PAIRS)):
            part = pl.ds(n * W, W)
            pltpu.make_async_copy(buf.at[part], out.at[part], osem.at[n]).start()
        for n in range(len(PAIRS)):
            part = pl.ds(n * W, W)
            pltpu.make_async_copy(buf.at[part], out.at[part], osem.at[n]).wait()

    size = len(PAIRS) * W
    return call(
        kernel,
        after,
        [table],
        [child, front],
        [(size, W)],
        [
            pltpu.VMEM((size, W), jnp.float32),
            pltpu.VMEM((BLK, NP * W), jnp.float32),
            pltpu.SemaphoreType.DMA((blocks,)),
            pltpu.SemaphoreType.DMA((len(PAIRS),)),
        ],
    )


def block_tables(mapping, group):
    total = mapping.shape[0]
    ids = jnp.arange(total, dtype=jnp.int32)
    inverse = jnp.sum(jnp.where(mapping[:, None] == ids[None, :], ids[:, None], 0), axis=0)
    target = mapping // group
    same = (
        (ids[:, None] // group == ids[None, :] // group)
        & (target[:, None] == target[None, :])
        & (ids[None, :] < ids[:, None])
    )
    return inverse, target, jnp.sum(same.astype(jnp.int32), axis=1)


def halves(mine, theirs, sib):
    low = jnp.where(sib == 0, mine, theirs)
    high = jnp.where(sib == 0, theirs, mine)
    return low, high


def local(front, child_updates, child_map, pivot_inverses):
    n_row, n_col = lax.axis_size("row"), lax.axis_size("col")
    row, col, sib = lax.axis_index("row"), lax.axis_index("col"), lax.axis_index("sib")
    rows, cols = front.shape
    child = child_updates[0]
    group, cgroup, per = rows // BLK, cols // BLK, child.shape[0] // BLK
    capacity = group // n_row
    pivots = NP * W
    swap = [(0, 1), (1, 0)]

    inverse, target, rank = block_tables(child_map[0], group)
    shift_to = (col + jnp.arange(n_col, dtype=jnp.int32)) % n_col
    column_table = inverse.reshape(n_col, cgroup)[shift_to].reshape(-1)
    ids = jnp.arange(group, dtype=jnp.int32)
    own = row * group + ids
    slot = target[own] * capacity + rank[own]
    source = jnp.sum(jnp.where(slot[None, :] == ids[:, None], ids[None, :], 0), axis=1)
    codes = (col - source // per) % n_col * per + source % per
    arriving = inverse[own]
    place = arriving // group * capacity + rank[arriving]
    place_other = lax.ppermute(place, "sib", swap)
    place_tables = jnp.concatenate([place, place_other, sib[None].astype(jnp.int32)])

    pivot_ids = jnp.arange(pivots // BLK, dtype=jnp.int32)
    at = inverse[pivot_ids] - (row * n_col + col) * per
    first_device = ((row == 0) & (col == 0) & (sib == 0)).astype(jnp.int32)
    corner_table = jnp.concatenate(
        [
            jnp.where((at >= 0) & (at < per), at, -1),
            inverse[pivot_ids],
            first_device[None],
        ]
    )

    count = len(CHUNKS)
    starts = [sum(CHUNKS[:j]) for j in range(count)]
    widths = [blocks * BLK for blocks in CHUNKS]
    token = jnp.zeros(TOKEN, jnp.float32)
    received, outgoing, A = [], [], []
    ring = [[(i, (i + s) % n_col) for i in range(n_col)] for s in range(n_col)]
    bits = n_col.bit_length() - 1
    path = [i ^ (i >> 1) for i in range(n_col)]
    mirror = [sum((q >> b & 1) << bits - 1 - b for b in range(bits)) for q in path]
    along, place_on_path = [], jnp.zeros((), jnp.int32)
    for core, way in enumerate((path, mirror)):
        along += [(core * n_col + way[i], core * n_col + way[i + 1]) for i in range(n_col - 1)]
        for i, q in enumerate(way):
            place_on_path = place_on_path + jnp.where((sib == core) & (col == q), i, 0)
    upward = [(i, i + 1) for i in range(n_row - 1)]
    half_own = rows // 2
    row_ids = row * rows + jnp.arange(rows, dtype=jnp.int32)

    def split(j):
        nonlocal token
        *parts, token = split_columns([token], child, column_table, starts[j], CHUNKS[j], n_col)
        moved = [lax.ppermute(parts[s], "col", ring[s]) for s in range(1, n_col)]
        received.append([parts[0]] + moved)

    def arrange(j):
        nonlocal token
        ordered, token = order_rows([token], received[j], codes)
        mine = lax.all_to_all(
            ordered.reshape(n_row, -1, widths[j]), "row", split_axis=0, concat_axis=0, tiled=True
        ).reshape(rows, widths[j])
        outgoing.append(mine)

    def swap_children(j):
        nonlocal token
        waits = row_waits[-1:] if j < count - 1 else []
        waits += panel_waits[j - 3 : j - 2 if j > 2 else 0]
        if row_wave[0] is not None:
            row_waits.append(row_wave[0])
            panel_waits.append(panel_wave[0])
        mine, token = hold([token, *waits], outgoing[j])
        outgoing[j] = (mine, lax.ppermute(mine, "sib", swap))

    def join(mine):
        low, high = halves(mine, lax.ppermute(mine, "sib", swap), sib)
        return low, high

    panels, rows_held = [], []
    panel_wave, row_wave, row_waits, panel_waits = [None], [None], [], []
    own_panels = []

    def send_panel(j):
        value = row_wave_panel(j) if j < NP else panel_wave[0]
        if panel_wave[0] is not None and j < NP:
            value = jnp.where(col == 0, value, panel_wave[0])
        panels.append(value)
        panel_wave[0] = lax.ppermute(value, ("sib", "col"), along)

    def row_wave_panel(j):
        work = lax.dynamic_slice_in_dim(A[j], sib * half_own, half_own, 0)
        ids = lax.dynamic_slice_in_dim(row_ids, sib * half_own, half_own, 0)
        for k in range(j):
            masked = jnp.where((ids >= (k + 1) * W)[:, None], own_panels[k], 0.0)
            work = work - dot(masked, corner_upper(k, j), TRAIL)
        own_panels.append(dot(work, pivot_inverses[j], PANEL))
        return own_panels[j]

    def corner_upper(k, j):
        if k == 0:
            return corner[0, j]
        return corner[1, 2] - dot(lower_corner(0, 1), corner[0, 2], TRAIL)

    def lower_corner(k, j):
        if k == 0:
            return dot(corner[j, 0], pivot_inverses[0], PANEL)
        work = corner[2, 1] - dot(lower_corner(0, 2), corner[0, 1], TRAIL)
        return dot(work, pivot_inverses[1], PANEL)

    def send_rows(j, half):
        live = [i for i in range(j - n_row + 1, j + 1) if 0 <= i < count]
        width = max(widths[i] for i in live)
        wave = row_wave[0]
        if half is not None and half.shape[1] < width:
            half = jnp.pad(half, ((0, 0), (0, width - half.shape[1])))
        if wave is not None:
            wave = wave[:, :width]
            if half is not None:
                wave = jnp.where(row == 0, half, wave)
        else:
            wave = half
        rows_held.append(wave)
        live = [i for i in live if i > j - n_row + 1]
        if live:
            width = max(widths[i] for i in live)
            row_wave[0] = lax.ppermute(wave[:, :width], "row", upward)

    def place_blocks(j):
        nonlocal token
        whole, half, token = assemble(
            [token], front, *outgoing[j], place_tables, starts[j] * BLK, pivots // 2
        )
        A.append(whole)
        send_rows(j, half)
        if j < NP + n_col - 2:
            send_panel(j)

    split(0)
    share, token = corner_share([token], child, front, corner_table)
    everywhere = ("sib", "row", "col")
    share = lax.psum_scatter(share, everywhere, scatter_dimension=0, tiled=True)
    share = lax.all_gather(share, everywhere, axis=0, tiled=True)
    corner = {pair: share[n * W : (n + 1) * W] for n, pair in enumerate(PAIRS)}
    split(1)
    arrange(0)
    split(2)
    arrange(1)
    swap_children(0)
    for j in range(count):
        if j + 3 < count:
            split(j + 3)
        if j + 2 < count:
            arrange(j + 2)
        place_blocks(j)
        if j + 1 < count:
            swap_children(j + 1)
    panels.append(panel_wave[0])
    for j in range(count, count + n_row - 1):
        send_rows(j, None)

    def pick(held, where_here, steps, width):
        value = held[0][:, :width]
        for i in range(1, steps):
            value = jnp.where(where_here == i, held[i][:, :width], value)
        return value

    half_ids = lax.dynamic_slice_in_dim(row_ids, sib * half_own, half_own, 0)
    lower, final = [], []
    for k in range(NP):
        final.append(pick(panels[k:], place_on_path, n_col, W))
        lower.append(jnp.where((half_ids >= (k + 1) * W)[:, None], final[k], 0.0))
    below = {(k, c): lower_corner(k, c) for k in range(NP) for c in range(k + 1, NP)}

    outs = []
    for j in range(count):
        low, high = join(pick(rows_held[j:], row, n_row, widths[j]))
        raw = jnp.concatenate([low, high], axis=0)
        R = [raw[k * W : (k + 1) * W] for k in range(NP)]
        for k in range(NP):
            for later in range(k + 1, NP):
                R[later] = R[later] - dot(below[k, later], R[k], TRAIL)
        value = lax.dynamic_slice_in_dim(A[j], sib * half_own, half_own, 0)
        for some in (slice(0, NP - 1), slice(NP - 1, NP)):
            value = value - dot(
                jnp.concatenate(lower[some], axis=1), jnp.concatenate(R[some], axis=0), TRAIL
            )
        if j < NP:
            value = jnp.where(col == 0, final[j], value)
        outs.append(jnp.concatenate(join(value), axis=0))
    return jnp.concatenate(outs, axis=1)


def spread(value, axis, source):
    kept = jnp.where(lax.axis_index(axis) == source, value, 0).astype(value.dtype)
    return lax.psum(kept, axis)


def plain_local(front, child_updates, child_map, pivot_inverses):
    row_count = lax.axis_size("row")
    row_here = lax.axis_index("row")
    col_here = lax.axis_index("col")
    sib_here = lax.axis_index("sib")
    rows_dev, cols_dev = front.shape
    group_blocks = rows_dev // BLK
    total_blocks = child_map.shape[1]
    capacity = max(1, group_blocks * group_blocks // total_blocks)
    inverse_map, target_group, rank_of = block_tables(child_map[0], group_blocks)
    columns = jnp.arange(F, dtype=jnp.int32)
    column_source = inverse_map[columns // BLK] * BLK + columns % BLK
    permuted = jnp.take(child_updates[0], column_source, axis=1)
    group_rows = lax.all_to_all(permuted, "col", split_axis=1, concat_axis=0, tiled=True)
    local_blocks = group_rows.reshape(group_blocks, BLK, cols_dev)
    local_ids = jnp.arange(group_blocks, dtype=jnp.int32)
    own_blocks = row_here * group_blocks + local_ids
    send_slot = target_group[own_blocks] * capacity + rank_of[own_blocks]
    slot_ids = jnp.arange(row_count * capacity, dtype=jnp.int32)
    slot_hits = send_slot[None, :] == slot_ids[:, None]
    source_block = jnp.sum(jnp.where(slot_hits, local_ids[None, :], 0), axis=1)
    filled = jnp.any(slot_hits, axis=1)
    outgoing = jnp.where(filled[:, None, None], jnp.take(local_blocks, source_block, axis=0), 0.0)
    incoming = lax.all_to_all(
        outgoing.reshape(row_count * capacity * BLK, cols_dev),
        "row",
        split_axis=0,
        concat_axis=0,
        tiled=True,
    )
    arriving = inverse_map[own_blocks]
    receive_slot = arriving // group_blocks * capacity + rank_of[arriving]
    relocated = jnp.take(
        incoming.reshape(row_count * capacity, BLK, cols_dev), receive_slot, axis=0
    ).reshape(rows_dev, cols_dev)
    half_rows = rows_dev // 2
    working = lax.psum_scatter(
        relocated, "sib", scatter_dimension=0, tiled=True
    ) + lax.dynamic_slice_in_dim(front, sib_here * half_rows, half_rows, 0)
    row_start = row_here * rows_dev + sib_here * half_rows
    global_rows = row_start + jnp.arange(working.shape[0], dtype=jnp.int32)
    global_cols = col_here * cols_dev + jnp.arange(cols_dev, dtype=jnp.int32)
    for panel_index in range(NP):
        first_col = panel_index * W
        after_panel = first_col + W
        col_root = first_col // cols_dev
        col_offset = first_col % cols_dev
        pivot_cols = working[:, col_offset : col_offset + W]
        pivot_cols = spread(pivot_cols, "col", col_root)
        group_offset = first_col % rows_dev
        row_root = group_offset // half_rows * row_count + first_col // rows_dev
        row_offset = group_offset % half_rows
        pivot_rows = spread(working[row_offset : row_offset + W, :], ("sib", "row"), row_root)
        panel_block = jnp.dot(
            pivot_cols,
            pivot_inverses[panel_index],
            precision=lax.Precision.HIGHEST,
            preferred_element_type=jnp.float32,
        )
        update = jnp.dot(
            panel_block,
            pivot_rows,
            precision=lax.Precision.HIGHEST,
            preferred_element_type=jnp.float32,
        )
        inside = (global_rows >= after_panel)[:, None] & (global_cols >= after_panel)[None, :]
        working = working - jnp.where(inside, update, 0.0)
        placed = lax.dynamic_update_slice(working, panel_block, (0, col_offset))
        working = jnp.where(col_here == col_root, placed, working)
    working = lax.all_gather(working, "sib", axis=0, tiled=True)
    return working

def solution(mesh):
    placed = (P("row", "col"), P("sib", ("row", "col"), None), P("sib", None), P())
    rows, cols = F // mesh.shape["row"], F // mesh.shape["col"]
    wide = rows >= NP * W and cols == sum(CHUNKS) * BLK and mesh.shape["sib"] == 2
    return jax.shard_map(
        local if wide else plain_local,
        mesh=mesh,
        in_specs=placed,
        out_specs=P("row", "col"),
        check_vma=False,
    )
```

```python
import jax
import jax.numpy as jnp
from jax import lax
from jax.experimental import pallas as pl
from jax.experimental.pallas import tpu as pltpu
from jax.sharding import PartitionSpec as P

F = 8192
W = 512
BLK = 128
NP = 3
CHUNKS = (4, 4, 4, 3, 1)
VMEM_LIMIT = 48 * 1024 * 1024
TRAIL = lax.Precision.HIGH
PANEL = lax.Precision.HIGHEST


def dot(a, b, precision):
    return jnp.dot(a, b, precision=precision, preferred_element_type=jnp.float32)


TOKEN = (8, 128)


def call(kernel, after, tables, arrays, outs, scratch):
    def ordered(*refs):
        n = len(tables) + len(arrays)
        m = n + len(after)
        kernel(*refs[:n], *refs[m : m + len(outs)], *refs[m + 1 + len(outs) :])

    return pl.pallas_call(
        ordered,
        out_shape=[jax.ShapeDtypeStruct(shape, jnp.float32) for shape in (*outs, TOKEN)],
        in_specs=[pl.BlockSpec(memory_space=pltpu.SMEM)] * len(tables)
        + [pl.BlockSpec(memory_space=pl.ANY)] * (len(arrays) + len(after)),
        out_specs=[pl.BlockSpec(memory_space=pl.ANY)] * (len(outs) + 1),
        scratch_shapes=scratch,
        compiler_params=pltpu.CompilerParams(vmem_limit_bytes=VMEM_LIMIT),
        cost_estimate=pl.CostEstimate(flops=0, bytes_accessed=4096, transcendentals=0),
    )(*tables, *arrays, *after)


def hold(after, value):
    def kernel(*refs):
        pass

    return pl.pallas_call(
        kernel,
        out_shape=[
            jax.ShapeDtypeStruct(value.shape, jnp.float32),
            jax.ShapeDtypeStruct(TOKEN, jnp.float32),
        ],
        in_specs=[pl.BlockSpec(memory_space=pl.ANY)] * (1 + len(after)),
        out_specs=[pl.BlockSpec(memory_space=pl.ANY)] * 2,
        input_output_aliases={0: 0},
        cost_estimate=pl.CostEstimate(flops=0, bytes_accessed=4096, transcendentals=0),
    )(value, *after)


def split_columns(after, child, table, first, count, parts):
    rows = child.shape[0]
    stride = table.shape[0] // parts

    def kernel(table_ref, child_ref, *rest):
        outs, (buf, sems, osems) = rest[:parts], rest[parts:]
        into, back = [], []
        for part in range(parts):
            for b in range(count):
                source = pl.multiple_of(table_ref[part * stride + first + b] * BLK, BLK)
                into.append(
                    pltpu.make_async_copy(
                        child_ref.at[:, pl.ds(source, BLK)],
                        buf.at[part, :, pl.ds(b * BLK, BLK)],
                        sems.at[part * count + b],
                    )
                )
                into[-1].start()
        for part in range(parts):
            for b in range(count):
                into[part * count + b].wait()
            back.append(pltpu.make_async_copy(buf.at[part], outs[part], osems.at[part]))
            back[-1].start()
        for copy in back:
            copy.wait()

    return call(
        kernel,
        after,
        [table],
        [child],
        [(rows, count * BLK)] * parts,
        [
            pltpu.VMEM((parts, rows, count * BLK), jnp.float32),
            pltpu.SemaphoreType.DMA((parts * count,)),
            pltpu.SemaphoreType.DMA((parts,)),
        ],
    )


def order_rows(after, sources, codes):
    rows, width = sources[0].shape
    per = rows // BLK
    total = codes.shape[0]

    def kernel(code_ref, *rest):
        ins, (out, buf, sems, osems) = rest[: len(sources)], rest[len(sources) :]
        for o in range(total):
            code = code_ref[o]
            which = code // per
            start = pl.multiple_of((code % per) * BLK, BLK)
            for s in range(len(sources)):

                @pl.when(which == s)
                def _(s=s, o=o, start=start):
                    pltpu.make_async_copy(
                        ins[s].at[pl.ds(start, BLK)], buf.at[pl.ds(o * BLK, BLK)], sems.at[o]
                    ).start()

        back = []
        for o in range(total):
            here = pl.ds(o * BLK, BLK)
            pltpu.make_async_copy(ins[0].at[pl.ds(0, BLK)], buf.at[here], sems.at[o]).wait()
            back.append(pltpu.make_async_copy(buf.at[here], out.at[here], osems.at[o]))
            back[-1].start()
        for copy in back:
            copy.wait()

    return call(
        kernel,
        after,
        [codes],
        list(sources),
        [(total * BLK, width)],
        [
            pltpu.VMEM((total * BLK, width), jnp.float32),
            pltpu.SemaphoreType.DMA((total,)),
            pltpu.SemaphoreType.DMA((total,)),
        ],
    )


def assemble(after, front, own, other, tables, first, half_rows):
    rows, width = own.shape
    blocks = rows // BLK

    def kernel(table_ref, front_ref, own_ref, other_ref, out, half, fbuf, abuf, bbuf, sems, osem):
        def copies(o):
            here = pl.ds(o * BLK, BLK)
            a = pl.multiple_of(table_ref[o] * BLK, BLK)
            b = pl.multiple_of(table_ref[blocks + o] * BLK, BLK)
            return (
                pltpu.make_async_copy(
                    front_ref.at[here, pl.ds(first, width)], fbuf.at[here], sems.at[0, o]
                ),
                pltpu.make_async_copy(own_ref.at[pl.ds(a, BLK)], abuf.at[here], sems.at[1, o]),
                pltpu.make_async_copy(other_ref.at[pl.ds(b, BLK)], bbuf.at[here], sems.at[2, o]),
            )

        for o in range(blocks):
            for copy in copies(o):
                copy.start()
        back = []
        for o in range(blocks):
            for copy in copies(o):
                copy.wait()
            here = pl.ds(o * BLK, BLK)
            fbuf[here, :] = (abuf[here, :] + bbuf[here, :]) + fbuf[here, :]
            back.append(pltpu.make_async_copy(fbuf.at[here], out.at[here], sems.at[0, o]))
            back[-1].start()
        mine = pl.multiple_of(table_ref[2 * blocks] * half_rows, BLK)
        last = pltpu.make_async_copy(fbuf.at[pl.ds(mine, half_rows)], half, osem)
        last.start()
        for copy in back:
            copy.wait()
        last.wait()

    return call(
        kernel,
        after,
        [tables],
        [front, own, other],
        [(rows, width), (half_rows, width)],
        [pltpu.VMEM((rows, width), jnp.float32)] * 3
        + [pltpu.SemaphoreType.DMA((3, blocks)), pltpu.SemaphoreType.DMA],
    )


PAIRS = [(0, 1), (0, 2), (1, 0), (1, 2), (2, 0), (2, 1)]
WB = W // BLK


def corner_share(after, child, front, table):
    per = child.shape[0] // BLK
    blocks = NP * WB

    def kernel(table_ref, child_ref, front_ref, out, buf, strip, sem, osem):
        holder = table_ref[2 * blocks] == 1

        def front_copy(n):
            k, c = PAIRS[n]
            return pltpu.make_async_copy(
                front_ref.at[pl.ds(k * W, W), pl.ds(c * W, W)], buf.at[pl.ds(n * W, W)], osem.at[n]
            )

        @pl.when(holder)
        def _():
            for n in range(len(PAIRS)):
                front_copy(n).start()
            for n in range(len(PAIRS)):
                front_copy(n).wait()

        @pl.when(jnp.logical_not(holder))
        def _():
            for n in range(len(PAIRS)):
                buf[n * W : (n + 1) * W, :] = jnp.zeros((W, W), jnp.float32)

        def add_row(p, carry):
            here = table_ref[p]

            @pl.when(here >= 0)
            def _():
                start = pl.multiple_of(here * BLK, BLK)
                copies = []
                for b in range(blocks):
                    source = pl.multiple_of(table_ref[blocks + b] * BLK, BLK)
                    copies.append(
                        pltpu.make_async_copy(
                            child_ref.at[pl.ds(start, BLK), pl.ds(source, BLK)],
                            strip.at[:, pl.ds(b * BLK, BLK)],
                            sem.at[b],
                        )
                    )
                    copies[-1].start()
                for copy in copies:
                    copy.wait()
                k = p // WB
                inner = pl.multiple_of((p % WB) * BLK, BLK)
                for n, (mine, c) in enumerate(PAIRS):

                    @pl.when(k == mine)
                    def _(n=n, c=c):
                        rows = pl.ds(n * W + inner, BLK)
                        buf[rows, :] = buf[rows, :] + strip[:, c * W : (c + 1) * W]

            return carry

        lax.fori_loop(0, blocks, add_row, 0)
        for n in range(len(PAIRS)):
            part = pl.ds(n * W, W)
            pltpu.make_async_copy(buf.at[part], out.at[part], osem.at[n]).start()
        for n in range(len(PAIRS)):
            part = pl.ds(n * W, W)
            pltpu.make_async_copy(buf.at[part], out.at[part], osem.at[n]).wait()

    size = len(PAIRS) * W
    return call(
        kernel,
        after,
        [table],
        [child, front],
        [(size, W)],
        [
            pltpu.VMEM((size, W), jnp.float32),
            pltpu.VMEM((BLK, NP * W), jnp.float32),
            pltpu.SemaphoreType.DMA((blocks,)),
            pltpu.SemaphoreType.DMA((len(PAIRS),)),
        ],
    )


def block_tables(mapping, group):
    total = mapping.shape[0]
    ids = jnp.arange(total, dtype=jnp.int32)
    inverse = jnp.sum(jnp.where(mapping[:, None] == ids[None, :], ids[:, None], 0), axis=0)
    target = mapping // group
    same = (
        (ids[:, None] // group == ids[None, :] // group)
        & (target[:, None] == target[None, :])
        & (ids[None, :] < ids[:, None])
    )
    return inverse, target, jnp.sum(same.astype(jnp.int32), axis=1)


def halves(mine, theirs, sib):
    low = jnp.where(sib == 0, mine, theirs)
    high = jnp.where(sib == 0, theirs, mine)
    return low, high


def local(front, child_updates, child_map, pivot_inverses):
    n_row, n_col = lax.axis_size("row"), lax.axis_size("col")
    row, col, sib = lax.axis_index("row"), lax.axis_index("col"), lax.axis_index("sib")
    rows, cols = front.shape
    child = child_updates[0]
    group, cgroup, per = rows // BLK, cols // BLK, child.shape[0] // BLK
    capacity = group // n_row
    pivots = NP * W
    swap = [(0, 1), (1, 0)]

    inverse, target, rank = block_tables(child_map[0], group)
    shift_to = (col + jnp.arange(n_col, dtype=jnp.int32)) % n_col
    column_table = inverse.reshape(n_col, cgroup)[shift_to].reshape(-1)
    ids = jnp.arange(group, dtype=jnp.int32)
    own = row * group + ids
    slot = target[own] * capacity + rank[own]
    source = jnp.sum(jnp.where(slot[None, :] == ids[:, None], ids[None, :], 0), axis=1)
    codes = (col - source // per) % n_col * per + source % per
    arriving = inverse[own]
    place = arriving // group * capacity + rank[arriving]
    place_other = lax.ppermute(place, "sib", swap)
    place_tables = jnp.concatenate([place, place_other, sib[None].astype(jnp.int32)])

    pivot_ids = jnp.arange(pivots // BLK, dtype=jnp.int32)
    at = inverse[pivot_ids] - (row * n_col + col) * per
    first_device = ((row == 0) & (col == 0) & (sib == 0)).astype(jnp.int32)
    corner_table = jnp.concatenate(
        [
            jnp.where((at >= 0) & (at < per), at, -1),
            inverse[pivot_ids],
            first_device[None],
        ]
    )

    count = len(CHUNKS)
    starts = [sum(CHUNKS[:j]) for j in range(count)]
    widths = [blocks * BLK for blocks in CHUNKS]
    token = jnp.zeros(TOKEN, jnp.float32)
    received, outgoing, A = [], [], []
    ring = [[(i, (i + s) % n_col) for i in range(n_col)] for s in range(n_col)]
    bits = n_col.bit_length() - 1
    path = [i ^ (i >> 1) for i in range(n_col)]
    mirror = [sum((q >> b & 1) << bits - 1 - b for b in range(bits)) for q in path]
    along, place_on_path = [], jnp.zeros((), jnp.int32)
    for core, way in enumerate((path, mirror)):
        along += [(core * n_col + way[i], core * n_col + way[i + 1]) for i in range(n_col - 1)]
        for i, q in enumerate(way):
            place_on_path = place_on_path + jnp.where((sib == core) & (col == q), i, 0)
    upward = [(i, i + 1) for i in range(n_row - 1)]
    half_own = rows // 2
    row_ids = row * rows + jnp.arange(rows, dtype=jnp.int32)

    def split(j):
        nonlocal token
        *parts, token = split_columns([token], child, column_table, starts[j], CHUNKS[j], n_col)
        moved = [lax.ppermute(parts[s], "col", ring[s]) for s in range(1, n_col)]
        received.append([parts[0]] + moved)

    def arrange(j):
        nonlocal token
        ordered, token = order_rows([token], received[j], codes)
        mine = lax.all_to_all(
            ordered.reshape(n_row, -1, widths[j]), "row", split_axis=0, concat_axis=0, tiled=True
        ).reshape(rows, widths[j])
        outgoing.append(mine)

    def swap_children(j):
        nonlocal token
        waits = row_waits[-1:] if j < count - 1 else []
        waits += panel_waits[j - 3 : j - 2 if j > 2 else 0]
        if row_wave[0] is not None:
            row_waits.append(row_wave[0])
            panel_waits.append(panel_wave[0])
        mine, token = hold([token, *waits], outgoing[j])
        outgoing[j] = (mine, lax.ppermute(mine, "sib", swap))

    def join(mine):
        low, high = halves(mine, lax.ppermute(mine, "sib", swap), sib)
        return low, high

    panels, rows_held = [], []
    panel_wave, row_wave, row_waits, panel_waits = [None], [None], [], []
    own_panels = []

    def send_panel(j):
        value = row_wave_panel(j) if j < NP else panel_wave[0]
        if panel_wave[0] is not None and j < NP:
            value = jnp.where(col == 0, value, panel_wave[0])
        panels.append(value)
        panel_wave[0] = lax.ppermute(value, ("sib", "col"), along)

    def row_wave_panel(j):
        work = lax.dynamic_slice_in_dim(A[j], sib * half_own, half_own, 0)
        ids = lax.dynamic_slice_in_dim(row_ids, sib * half_own, half_own, 0)
        for k in range(j):
            masked = jnp.where((ids >= (k + 1) * W)[:, None], own_panels[k], 0.0)
            work = work - dot(masked, corner_upper(k, j), TRAIL)
        own_panels.append(dot(work, pivot_inverses[j], PANEL))
        return own_panels[j]

    def corner_upper(k, j):
        if k == 0:
            return corner[0, j]
        return corner[1, 2] - dot(lower_corner(0, 1), corner[0, 2], TRAIL)

    def lower_corner(k, j):
        if k == 0:
            return dot(corner[j, 0], pivot_inverses[0], PANEL)
        work = corner[2, 1] - dot(lower_corner(0, 2), corner[0, 1], TRAIL)
        return dot(work, pivot_inverses[1], PANEL)

    def send_rows(j, half):
        live = [i for i in range(j - n_row + 1, j + 1) if 0 <= i < count]
        width = max(widths[i] for i in live)
        wave = row_wave[0]
        if half is not None and half.shape[1] < width:
            half = jnp.pad(half, ((0, 0), (0, width - half.shape[1])))
        if wave is not None:
            wave = wave[:, :width]
            if half is not None:
                wave = jnp.where(row == 0, half, wave)
        else:
            wave = half
        rows_held.append(wave)
        live = [i for i in live if i > j - n_row + 1]
        if live:
            width = max(widths[i] for i in live)
            row_wave[0] = lax.ppermute(wave[:, :width], "row", upward)

    def place_blocks(j):
        nonlocal token
        whole, half, token = assemble(
            [token], front, *outgoing[j], place_tables, starts[j] * BLK, pivots // 2
        )
        A.append(whole)
        send_rows(j, half)
        if j < NP + n_col - 2:
            send_panel(j)

    split(0)
    share, token = corner_share([token], child, front, corner_table)
    everywhere = ("sib", "row", "col")
    share = lax.psum_scatter(share, everywhere, scatter_dimension=0, tiled=True)
    share = lax.all_gather(share, everywhere, axis=0, tiled=True)
    corner = {pair: share[n * W : (n + 1) * W] for n, pair in enumerate(PAIRS)}
    split(1)
    arrange(0)
    split(2)
    arrange(1)
    swap_children(0)
    for j in range(count):
        if j + 3 < count:
            split(j + 3)
        if j + 2 < count:
            arrange(j + 2)
        place_blocks(j)
        if j + 1 < count:
            swap_children(j + 1)
    panels.append(panel_wave[0])
    for j in range(count, count + n_row - 1):
        send_rows(j, None)

    def pick(held, where_here, steps, width):
        value = held[0][:, :width]
        for i in range(1, steps):
            value = jnp.where(where_here == i, held[i][:, :width], value)
        return value

    half_ids = lax.dynamic_slice_in_dim(row_ids, sib * half_own, half_own, 0)
    lower, final = [], []
    for k in range(NP):
        final.append(pick(panels[k:], place_on_path, n_col, W))
        lower.append(jnp.where((half_ids >= (k + 1) * W)[:, None], final[k], 0.0))
    below = {(k, c): lower_corner(k, c) for k in range(NP) for c in range(k + 1, NP)}

    outs = []
    for j in range(count):
        low, high = join(pick(rows_held[j:], row, n_row, widths[j]))
        raw = jnp.concatenate([low, high], axis=0)
        R = [raw[k * W : (k + 1) * W] for k in range(NP)]
        for k in range(NP):
            for later in range(k + 1, NP):
                R[later] = R[later] - dot(below[k, later], R[k], TRAIL)
        value = lax.dynamic_slice_in_dim(A[j], sib * half_own, half_own, 0)
        for some in (slice(0, NP - 1), slice(NP - 1, NP)):
            value = value - dot(
                jnp.concatenate(lower[some], axis=1), jnp.concatenate(R[some], axis=0), TRAIL
            )
        if j < NP:
            value = jnp.where(col == 0, final[j], value)
        outs.append(jnp.concatenate(join(value), axis=0))
    return jnp.concatenate(outs, axis=1)


def spread(value, axis, source):
    kept = jnp.where(lax.axis_index(axis) == source, value, 0).astype(value.dtype)
    return lax.psum(kept, axis)


def plain_local(front, child_updates, child_map, pivot_inverses):
    row_count = lax.axis_size("row")
    row_here = lax.axis_index("row")
    col_here = lax.axis_index("col")
    sib_here = lax.axis_index("sib")
    rows_dev, cols_dev = front.shape
    group_blocks = rows_dev // BLK
    total_blocks = child_map.shape[1]
    capacity = max(1, group_blocks * group_blocks // total_blocks)
    inverse_map, target_group, rank_of = block_tables(child_map[0], group_blocks)
    columns = jnp.arange(F, dtype=jnp.int32)
    column_source = inverse_map[columns // BLK] * BLK + columns % BLK
    permuted = jnp.take(child_updates[0], column_source, axis=1)
    group_rows = lax.all_to_all(permuted, "col", split_axis=1, concat_axis=0, tiled=True)
    local_blocks = group_rows.reshape(group_blocks, BLK, cols_dev)
    local_ids = jnp.arange(group_blocks, dtype=jnp.int32)
    own_blocks = row_here * group_blocks + local_ids
    send_slot = target_group[own_blocks] * capacity + rank_of[own_blocks]
    slot_ids = jnp.arange(row_count * capacity, dtype=jnp.int32)
    slot_hits = send_slot[None, :] == slot_ids[:, None]
    source_block = jnp.sum(jnp.where(slot_hits, local_ids[None, :], 0), axis=1)
    filled = jnp.any(slot_hits, axis=1)
    outgoing = jnp.where(filled[:, None, None], jnp.take(local_blocks, source_block, axis=0), 0.0)
    incoming = lax.all_to_all(
        outgoing.reshape(row_count * capacity * BLK, cols_dev),
        "row",
        split_axis=0,
        concat_axis=0,
        tiled=True,
    )
    arriving = inverse_map[own_blocks]
    receive_slot = arriving // group_blocks * capacity + rank_of[arriving]
    relocated = jnp.take(
        incoming.reshape(row_count * capacity, BLK, cols_dev), receive_slot, axis=0
    ).reshape(rows_dev, cols_dev)
    half_rows = rows_dev // 2
    working = lax.psum_scatter(
        relocated, "sib", scatter_dimension=0, tiled=True
    ) + lax.dynamic_slice_in_dim(front, sib_here * half_rows, half_rows, 0)
    row_start = row_here * rows_dev + sib_here * half_rows
    global_rows = row_start + jnp.arange(working.shape[0], dtype=jnp.int32)
    global_cols = col_here * cols_dev + jnp.arange(cols_dev, dtype=jnp.int32)
    for panel_index in range(NP):
        first_col = panel_index * W
        after_panel = first_col + W
        col_root = first_col // cols_dev
        col_offset = first_col % cols_dev
        pivot_cols = working[:, col_offset : col_offset + W]
        pivot_cols = spread(pivot_cols, "col", col_root)
        group_offset = first_col % rows_dev
        row_root = group_offset // half_rows * row_count + first_col // rows_dev
        row_offset = group_offset % half_rows
        pivot_rows = spread(working[row_offset : row_offset + W, :], ("sib", "row"), row_root)
        panel_block = jnp.dot(
            pivot_cols,
            pivot_inverses[panel_index],
            precision=lax.Precision.HIGHEST,
            preferred_element_type=jnp.float32,
        )
        update = jnp.dot(
            panel_block,
            pivot_rows,
            precision=lax.Precision.HIGHEST,
            preferred_element_type=jnp.float32,
        )
        inside = (global_rows >= after_panel)[:, None] & (global_cols >= after_panel)[None, :]
        working = working - jnp.where(inside, update, 0.0)
        placed = lax.dynamic_update_slice(working, panel_block, (0, col_offset))
        working = jnp.where(col_here == col_root, placed, working)
    working = lax.all_gather(working, "sib", axis=0, tiled=True)
    return working

def solution(mesh):
    placed = (P("row", "col"), P("sib", ("row", "col"), None), P("sib", None), P())
    rows, cols = F // mesh.shape["row"], F // mesh.shape["col"]
    wide = rows >= NP * W and cols == sum(CHUNKS) * BLK and mesh.shape["sib"] == 2
    return jax.shard_map(
        local if wide else plain_local,
        mesh=mesh,
        in_specs=placed,
        out_specs=P("row", "col"),
        check_vma=False,
    )
```
